256 devices in a mesh: chan: 16 (over x, z_lo), win: 16 (over z_hi, y, core).
Axes of the slice: x: 4, y: 4, z: 8 (z_hi: 2, z_lo: 4; z = z_hi * 4 + z_lo), core: 2. Of those that a mesh axis runs over, the one named last changes fastest.
Arguments:
- records: bfloat16 [64, 512, 1024], P('win', 'chan'), may hold values from -6 to 6
- live: int32 [512], P('chan'), may hold values 0 or 1
- band_limit: int32 [512], P('chan'), may hold values from 1 to 100
Outputs:
- correlations: float32 [512, 100, 257], P(('chan', 'win'))
The draws below stay inside these ranges and needn't reach their ends.
Inputs may be any that keep to these rules, and one draw needn't show every extreme that they name: A pair of channel c with channel c + k is used for 1 <= k <= band_limit[c].
All inputs are finite; a program needn't handle non-finite values. No bound on the sum of `live` on one device may be relied on, other than what follows from the above.
Results may differ from the reference program's by a relative error of at most 0.0041.
Values may be sent and summed in bfloat16 or wider, within the bound.
A program may use at most 128 MiB of HBM per device.

```python
import math
import jax
import jax.numpy as jnp
from jax import lax

NS = 1024
R = 100
HALF_LAG = 128
HALF_WIN = 32
CH_DEV = 32
CHANNELS = 512
WINS = 64


def touch_ends(array, key, smallest, largest):
    place = [jax.random.randint(jax.random.fold_in(key, axis), (), 0, length) for axis, length in enumerate(array.shape)]
    longest = array.shape.index(max(array.shape))
    next_to = place[:longest] + [(place[longest] + 1) % array.shape[longest]] + place[longest + 1:]
    return array.at[tuple(place)].set(smallest).at[tuple(next_to)].set(largest)


def level_of(own_key, dims, split, smallest, top_value):
    loudness = 1.0
    for position, shards_of in split:
        draws = jax.random.uniform(jax.random.fold_in(jax.random.fold_in(own_key, 6), position), (shards_of,), jnp.float32, smallest / len(split), top_value / len(split))
        loudness = loudness * jnp.repeat(jnp.exp(draws), dims[position] // shards_of).reshape((-1,) + (1,) * (len(dims) - 1 - position))
    return loudness


def scatter_about(own_key, dims, width, limit, split=(), held_as=jnp.bfloat16):
    result = jax.random.normal(own_key, dims, jnp.float32) * width
    if len(split) > 0:
        result = level_of(own_key, dims, split, -0.22, 0.18) * result
    return jnp.clip(result, min=-limit, max=limit).astype(held_as)


def setup_inputs(seed: int = 0) -> dict:
    keys = jax.random.split(jax.random.key(seed), 4)
    records = scatter_about(keys[0], (WINS, CHANNELS, NS), 1.0, 6.0, ((0, 16), (1, 16)))
    live = touch_ends((jax.random.randint(keys[1], (CHANNELS,), 0, 8) < 7).astype(jnp.int32), jax.random.fold_in(keys[1], 1), 0, 1)
    band_limit = touch_ends(jax.random.randint(keys[2], (CHANNELS,), 1, R + 1), jax.random.fold_in(keys[2], 1), 1, R).astype(jnp.int32)
    return dict(records=records, live=live, band_limit=band_limit)


def forward_table(samples):
    times = jnp.arange(samples, dtype=jnp.int32)[:, None]
    freqs = jnp.arange(1, samples // 2 + 1, dtype=jnp.int32)[None, :]
    phase = jnp.mod(times * freqs, samples).astype(jnp.float32) * (2.0 * math.pi / samples)
    return jnp.concatenate([jnp.cos(phase), -jnp.sin(phase)], axis=1)

def inverse_table(samples, half_lag, windows_all):
    freqs = jnp.arange(1, samples // 2 + 1, dtype=jnp.int32)[:, None]
    shifts = jnp.arange(2 * half_lag + 1, dtype=jnp.int32)[None, :] - half_lag
    phase = jnp.mod(freqs * shifts, samples).astype(jnp.float32) * (2.0 * math.pi / samples)
    factor = 2.0 / math.sqrt(samples * windows_all)
    return jnp.concatenate([jnp.cos(phase), -jnp.sin(phase)], axis=0) * factor

def smooth_table(bins, half_win):
    index = jnp.arange(bins, dtype=jnp.int32)
    near = jnp.abs(index[:, None] - index[None, :]) <= half_win
    return near.astype(jnp.float32) / (2 * half_win + 1)

def whiten(block, live, ftab, band):
    spec = jnp.einsum('...t,tj->...j', block.astype(jnp.float32), ftab, precision=lax.Precision.HIGHEST)
    bins = ftab.shape[1] // 2
    real, imag = (spec[..., :bins], spec[..., bins:])
    amplitude = jnp.sqrt(real * real + imag * imag)
    smooth = jnp.einsum('...f,fg->...g', amplitude, band, precision=lax.Precision.HIGHEST) + 1e-06
    factor = live.astype(jnp.float32)[:, None] / smooth
    return jnp.concatenate([real * factor, imag * factor], axis=-1).astype(jnp.bfloat16)

def window_cross(own, extended, offsets):
    rows = own.shape[0]
    partner = jax.vmap(lambda k: lax.dynamic_slice_in_dim(extended, k, rows, 0), out_axes=1)(offsets)
    bins = own.shape[-1] // 2
    a_re = own[:, None, :bins].astype(jnp.float32)
    a_im = own[:, None, bins:].astype(jnp.float32)
    b_re = partner[..., :bins]
    b_im = partner[..., bins:]
    real = a_re * b_re + a_im * b_im
    imag = a_im * b_re - a_re * b_im
    return jnp.concatenate([real, imag], axis=-1)

def pair_mask(limits, reach):
    offsets = jnp.arange(1, reach + 1, dtype=jnp.int32)
    return (offsets[None, :] <= limits[:, None]).astype(jnp.float32)

def reference(records, live, band_limit):
    ftab = forward_table(NS)
    band = smooth_table(NS // 2, HALF_WIN)
    itab = inverse_table(NS, HALF_LAG, WINS)
    whitened = lax.map(lambda block: whiten(block, live, ftab, band), records)
    padded = jnp.pad(whitened, ((0, 0), (0, R + CH_DEV), (0, 0)))
    offsets = jnp.arange(1, R + 1, dtype=jnp.int32)

    def one_block(number):
        start = (number * CH_DEV).astype(jnp.int32)
        own_all = lax.dynamic_slice_in_dim(padded, start, CH_DEV, 1)
        ext_all = lax.dynamic_slice_in_dim(padded, start, CH_DEV + R, 1)

        def add_window(w, total):
            return total + window_cross(own_all[w], ext_all[w], offsets)
        stack = lax.fori_loop(0, WINS, add_window, jnp.zeros((CH_DEV, R, NS), jnp.float32))
        limits = lax.dynamic_slice_in_dim(band_limit, start, CH_DEV, 0)
        stack = stack * pair_mask(limits, R)[:, :, None]
        return jnp.einsum('crj,jl->crl', stack, itab, precision=lax.Precision.HIGHEST)
    blocks = lax.map(one_block, jnp.arange(CHANNELS // CH_DEV, dtype=jnp.int32))
    return blocks.reshape(CHANNELS, R, 2 * HALF_LAG + 1)
```

```python
import math

import jax
import jax.numpy as jnp
import ml_dtypes
import numpy as np
from jax import lax
from jax.experimental import pallas as pl
from jax.experimental.pallas import tpu as pltpu
from jax.sharding import PartitionSpec as P

R = 100
HALF_LAG = 128
HALF_WIN = 32
SAMPLES = 1024
BINS = SAMPLES // 2
LAGS = 2 * HALF_LAG + 1
WINS_ALL = 64
CHANNELS = 512

Z_LO = 4
WIN = 16
PLANE = Z_LO * WIN
SLICE = BINS // PLANE
ROWS = 2 * SLICE
LANES = 128

MESH = pl.DeviceIdType.MESH
F32, BF16 = jnp.float32, jnp.bfloat16


def split(table, terms):
    parts, rest = [], table.astype(np.float64)
    for _ in range(terms):
        part = rest.astype(np.float32).astype(ml_dtypes.bfloat16)
        parts.append(part)
        rest = rest - part.astype(np.float64)
    return parts


def forward_tables(terms):
    freqs = np.arange(1, BINS + 1)[:, None]
    times = np.arange(SAMPLES)[None, :]
    phase = np.mod(freqs * times, SAMPLES) * (2.0 * math.pi / SAMPLES)
    return np.stack(split(np.concatenate([np.cos(phase), -np.sin(phase)], axis=0), terms))


def inverse_tables(terms):
    freqs = np.arange(1, BINS + 1)[:, None]
    shifts = np.arange(LAGS)[None, :] - HALF_LAG
    phase = np.mod(freqs * shifts, SAMPLES) * (2.0 * math.pi / SAMPLES)
    factor = 2.0 / math.sqrt(SAMPLES * WINS_ALL)
    real = (np.cos(phase) * factor).reshape(PLANE, SLICE, LAGS)
    imag = (-np.sin(phase) * factor).reshape(PLANE, SLICE, LAGS)
    table = np.concatenate([real, imag], axis=1).reshape(SAMPLES, LAGS)
    table = np.pad(table, ((0, 0), (0, 3 * LANES - LAGS)))
    return np.stack(split(table, terms))


def band_table():
    index = np.arange(BINS)
    return (np.abs(index[:, None] - index[None, :]) <= HALF_WIN).astype(ml_dtypes.bfloat16)


def dot(a, b, dims):
    return lax.dot_general(a, b, (dims, ((), ())), preferred_element_type=F32)


def whiten_kernel(x_ref, live_ref, tab_ref, band_ref, out_ref):
    x = x_ref[...]
    spec = dot(tab_ref[0], x, ((1,), (1,)))
    for term in range(1, tab_ref.shape[0]):
        spec = spec + dot(tab_ref[term], x, ((1,), (1,)))
    real, imag = spec[:BINS], spec[BINS:]
    amplitude = jnp.sqrt(real * real + imag * imag)
    high = amplitude.astype(BF16)
    low = (amplitude - high.astype(F32)).astype(BF16)
    near = dot(band_ref[...], high, ((1,), (0,))) + dot(band_ref[...], low, ((1,), (0,)))
    factor = live_ref[...] / (near * (1.0 / (2 * HALF_WIN + 1)) + 1e-06)
    real = (real * factor).reshape(PLANE, SLICE, LANES)
    imag = (imag * factor).reshape(PLANE, SLICE, LANES)
    out_ref[...] = jnp.concatenate([real, imag], axis=1).astype(BF16)


def whiten(x, live):
    tab, band = jnp.asarray(forward_tables(2)), jnp.asarray(band_table())
    return pl.pallas_call(
        whiten_kernel,
        out_shape=jax.ShapeDtypeStruct((PLANE, ROWS, LANES), BF16),
        in_specs=[pl.BlockSpec(memory_space=pltpu.VMEM)] * 4,
        out_specs=pl.BlockSpec(memory_space=pltpu.VMEM),
        compiler_params=pltpu.CompilerParams(vmem_limit_bytes=32 << 20),
        cost_estimate=pl.CostEstimate(flops=600_000_000, bytes_accessed=5_000_000, transcendentals=65536),
    )(x, live, tab, band)


def places():
    chan, win = lax.axis_index("chan"), lax.axis_index("win")
    z_lo = lax.rem(chan, Z_LO)
    return chan - z_lo, z_lo * WIN + win


def device(base, place):
    return {"chan": base + lax.div(place, WIN), "win": lax.rem(place, WIN)}


def spread_kernel(w_ref, near_ref, far_ref, send_sem, near_sem, far_sem, own_sem):
    base, me = places()
    has_left, has_right = base > 0, base < (CHANNELS // 32 - Z_LO)
    barrier = pltpu.get_barrier_semaphore()

    def greet(i, _):
        peer = lax.rem(me + i, PLANE)
        pl.semaphore_signal(barrier, inc=1, device_id=device(base, peer), device_id_type=MESH)
        return 0

    def greet_far(i, _):
        peer = lax.rem(me + i, PLANE)
        pl.semaphore_signal(barrier, inc=1, device_id=device(base + Z_LO, peer), device_id_type=MESH)
        return 0

    lax.fori_loop(1, PLANE, greet, 0)

    @pl.when(has_right)
    def _():
        lax.fori_loop(0, PLANE, greet_far, 0)

    pl.semaphore_wait(barrier, PLANE - 1 + PLANE * has_left.astype(jnp.int32))
    own = pltpu.make_async_copy(w_ref.at[me], near_ref.at[me], own_sem)
    own.start()

    def send(i, _):
        peer = lax.rem(me + i, PLANE)
        pltpu.make_async_remote_copy(
            src_ref=w_ref.at[peer], dst_ref=near_ref.at[me], send_sem=send_sem,
            recv_sem=near_sem, device_id=device(base, peer), device_id_type=MESH,
        ).start()
        return 0

    def send_far(i, _):
        peer = lax.rem(me + i, PLANE)
        pltpu.make_async_remote_copy(
            src_ref=w_ref.at[peer], dst_ref=far_ref.at[me], send_sem=send_sem,
            recv_sem=far_sem, device_id=device(base - Z_LO, peer), device_id_type=MESH,
        ).start()
        return 0

    lax.fori_loop(1, PLANE, send, 0)

    @pl.when(has_left)
    def _():
        lax.fori_loop(0, PLANE, send_far, 0)

    @pl.when(jnp.logical_not(has_right))
    def _():
        far_ref[...] = jnp.zeros_like(far_ref)

    own.wait()
    rest = near_ref.at[pl.ds(0, PLANE - 1)]
    pltpu.make_async_copy(rest, rest, near_sem).wait()

    @pl.when(has_right)
    def _():
        pltpu.make_async_copy(far_ref, far_ref, far_sem).wait()

    pltpu.make_async_copy(rest, rest, send_sem).wait()

    @pl.when(has_left)
    def _():
        pltpu.make_async_copy(far_ref, far_ref, send_sem).wait()


def spread(w):
    shape = jax.ShapeDtypeStruct((PLANE, ROWS, LANES), BF16)
    return pl.pallas_call(
        spread_kernel,
        out_shape=(shape, shape),
        in_specs=[pl.BlockSpec(memory_space=pltpu.VMEM)],
        out_specs=(pl.BlockSpec(memory_space=pltpu.VMEM),) * 2,
        scratch_shapes=[pltpu.SemaphoreType.DMA] * 4,
        compiler_params=pltpu.CompilerParams(collective_id=0, has_side_effects=True),
        cost_estimate=pl.CostEstimate(flops=0, bytes_accessed=1_000_000, transcendentals=0),
    )(w)


def regroup(parts):
    group = lax.broadcasted_iota(jnp.int32, parts[0].shape, 1) // 32
    for bit in range(2):
        step = 32 << bit
        upper = (group // (1 << bit)) % 2 == 1
        new = list(parts)
        for i in range(4):
            if i & (1 << bit):
                continue
            a, b = parts[i], parts[i | (1 << bit)]
            new[i] = jnp.where(upper, pltpu.roll(b, step, 1), a)
            new[i | (1 << bit)] = jnp.where(upper, b, pltpu.roll(a, LANES - step, 1))
        parts = new
    return parts


def stack_kernel(near_ref, far_ref, out_ref, t_ref, u_ref):
    def take(s, _):
        for p, ref in enumerate((near_ref, far_ref)):
            parts = regroup([ref[z * WIN + s].astype(F32) for z in range(Z_LO)])
            for w in range(4):
                at = pl.ds(pl.multiple_of((s * 4 + w) * SLICE, SLICE), SLICE)
                t_ref[p, 0, at] = parts[w][:SLICE]
                t_ref[p, 1, at] = parts[w][SLICE:]
        return 0

    lax.fori_loop(0, WIN, take, 0)
    rows = lax.broadcasted_iota(jnp.int32, (LANES, LANES), 0)
    lanes = lax.broadcasted_iota(jnp.int32, (LANES, LANES), 1)
    for f in range(SLICE):
        every = pl.ds(f, WINS_ALL, stride=SLICE)
        a_re, a_im = t_ref[0, 0, every], t_ref[0, 1, every]
        own = jnp.concatenate([a_re, a_im], axis=0).astype(BF16)
        turned = jnp.concatenate([a_im, -a_re], axis=0).astype(BF16)
        further = jnp.concatenate([t_ref[1, 0, every], t_ref[1, 1, every]], axis=0).astype(BF16)
        both = jnp.concatenate([own, further], axis=1)
        for part, left in enumerate((own, turned)):
            pairs = dot(left, both, ((0,), (0,)))
            pairs = jnp.where(lanes > rows, pairs[:, :LANES], pairs[:, LANES:])
            u_ref[pl.ds(part * SLICE + f, LANES, stride=ROWS)] = pairs
    out_ref[...] = u_ref[...].astype(BF16).reshape(out_ref.shape)


def stack(near, far):
    return pl.pallas_call(
        stack_kernel,
        out_shape=jax.ShapeDtypeStruct((PLANE, 2, ROWS, LANES), BF16),
        in_specs=[pl.BlockSpec(memory_space=pltpu.VMEM)] * 2,
        out_specs=pl.BlockSpec(memory_space=pltpu.VMEM),
        scratch_shapes=[
            pltpu.VMEM((2, 2, WINS_ALL * SLICE, LANES), F32),
            pltpu.VMEM((LANES * ROWS, LANES), F32),
        ],
        compiler_params=pltpu.CompilerParams(vmem_limit_bytes=32 << 20),
        cost_estimate=pl.CostEstimate(flops=140_000_000, bytes_accessed=1_000_000, transcendentals=0),
    )(near, far)


def collect_kernel(s_ref, out_ref, send_sem, recv_sem, own_sem):
    base, me = places()
    barrier = pltpu.get_barrier_semaphore()

    def greet(i, _):
        peer = lax.rem(me + i, PLANE)
        pl.semaphore_signal(barrier, inc=1, device_id=device(base, peer), device_id_type=MESH)
        return 0

    lax.fori_loop(1, PLANE, greet, 0)
    pl.semaphore_wait(barrier, PLANE - 1)
    own = pltpu.make_async_copy(s_ref.at[me], out_ref.at[me], own_sem)
    own.start()

    def send(i, _):
        peer = lax.rem(me + i, PLANE)
        pltpu.make_async_remote_copy(
            src_ref=s_ref.at[peer], dst_ref=out_ref.at[me], send_sem=send_sem,
            recv_sem=recv_sem, device_id=device(base, peer), device_id_type=MESH,
        ).start()
        return 0

    lax.fori_loop(1, PLANE, send, 0)
    own.wait()
    rest = out_ref.at[pl.ds(0, PLANE - 1)]
    pltpu.make_async_copy(rest, rest, recv_sem).wait()
    pltpu.make_async_copy(rest, rest, send_sem).wait()


def collect(s):
    return pl.pallas_call(
        collect_kernel,
        out_shape=jax.ShapeDtypeStruct(s.shape, BF16),
        in_specs=[pl.BlockSpec(memory_space=pltpu.VMEM)],
        out_specs=pl.BlockSpec(memory_space=pltpu.VMEM),
        scratch_shapes=[pltpu.SemaphoreType.DMA] * 3,
        compiler_params=pltpu.CompilerParams(collective_id=1, has_side_effects=True),
        cost_estimate=pl.CostEstimate(flops=0, bytes_accessed=1_000_000, transcendentals=0),
    )(s)


def inverse_kernel(place_ref, s_ref, tab_ref, out_ref):
    left = jnp.concatenate([s_ref[:, c].reshape(SAMPLES, LANES) for c in range(2)], axis=1)
    pairs = dot(left, tab_ref[0], ((0,), (0,)))
    for term in range(1, tab_ref.shape[0]):
        pairs = pairs + dot(left, tab_ref[term], ((0,), (0,)))
    offsets = lax.broadcasted_iota(jnp.int32, (R, LAGS), 0) + 1
    for c in range(2):
        rows = pairs[c * LANES:(c + 1) * LANES]
        kept = pltpu.roll(rows, LANES - 1 - c - place_ref[0], 0)[:R, :LAGS]
        out_ref[c] = jnp.where(offsets <= place_ref[1 + c], kept, 0.0)


def inverse(place, s):
    tab = jnp.asarray(inverse_tables(2))
    return pl.pallas_call(
        inverse_kernel,
        out_shape=jax.ShapeDtypeStruct((2, R, LAGS), F32),
        in_specs=[pl.BlockSpec(memory_space=pltpu.SMEM)] + [pl.BlockSpec(memory_space=pltpu.VMEM)] * 2,
        out_specs=pl.BlockSpec(memory_space=pltpu.VMEM),
        compiler_params=pltpu.CompilerParams(vmem_limit_bytes=32 << 20),
        cost_estimate=pl.CostEstimate(flops=400_000_000, bytes_accessed=2_000_000, transcendentals=0),
    )(place, s, tab)


def shards(records, live, band_limit):
    chan, win = lax.axis_index("chan"), lax.axis_index("win")
    live = jnp.tile(live.astype(F32), 4)[None, :]
    w = whiten(records.reshape(LANES, SAMPLES), live)
    near, far = spread(w)
    s = collect(stack(near, far))
    first = lax.rem(chan, Z_LO) * 32 + win * 2
    limits = lax.dynamic_slice_in_dim(band_limit, win * 2, 2)
    room = CHANNELS - 1 - (chan * 32 + win * 2 + jnp.arange(2, dtype=jnp.int32))
    limits = jnp.minimum(limits, room)
    place = jnp.concatenate([first[None], limits]).astype(jnp.int32)
    return inverse(place, s)


def solution(mesh):
    placed = (P("win", "chan", None), P("chan"), P("chan"))
    return jax.shard_map(
        shards,
        mesh=mesh,
        in_specs=placed,
        out_specs=P(("chan", "win"), None, None),
        check_vma=False,
    )
```

```python
import math

import jax
import jax.numpy as jnp
import ml_dtypes
import numpy as np
from jax import lax
from jax.experimental import pallas as pl
from jax.experimental.pallas import tpu as pltpu
from jax.sharding import PartitionSpec as P

R = 100
HALF_LAG = 128
HALF_WIN = 32
SAMPLES = 1024
BINS = SAMPLES // 2
LAGS = 2 * HALF_LAG + 1
WINS_ALL = 64
CHANNELS = 512

LAGS_PAD = 272
X, Z_LO, Z, YC = 4, 4, 8, 8
PLANE = Z * YC
SLICE = BINS // PLANE
ROWS = 2 * SLICE
LANES = 128

MESH = pl.DeviceIdType.MESH
F32, BF16 = jnp.float32, jnp.bfloat16


def split(table, terms):
    parts, rest = [], table.astype(np.float64)
    for _ in range(terms):
        part = rest.astype(np.float32).astype(ml_dtypes.bfloat16)
        parts.append(part)
        rest = rest - part.astype(np.float64)
    return parts


def forward_tables(terms):
    freqs = np.arange(1, BINS + 1)[:, None]
    times = np.arange(SAMPLES)[None, :]
    phase = np.mod(freqs * times, SAMPLES) * (2.0 * math.pi / SAMPLES)
    return np.stack(split(np.concatenate([np.cos(phase), -np.sin(phase)], axis=0), terms))


def inverse_tables(terms):
    freqs = np.arange(1, BINS + 1)[:, None]
    shifts = np.arange(LAGS)[None, :] - HALF_LAG
    phase = np.mod(freqs * shifts, SAMPLES) * (2.0 * math.pi / SAMPLES)
    factor = 2.0 / math.sqrt(SAMPLES * WINS_ALL)
    real = (np.cos(phase) * factor).reshape(PLANE, SLICE, LAGS)
    imag = (-np.sin(phase) * factor).reshape(PLANE, SLICE, LAGS)
    table = np.concatenate([real, imag], axis=1).reshape(SAMPLES, LAGS).T
    table = np.pad(table, ((0, LAGS_PAD - LAGS), (0, 0)))
    return np.stack(split(table, terms))


def band_table():
    index = np.arange(BINS)
    return (np.abs(index[:, None] - index[None, :]) <= HALF_WIN).astype(ml_dtypes.bfloat16)


def dot(a, b, dims):
    return lax.dot_general(a, b, (dims, ((), ())), preferred_element_type=F32)


def whiten(x, live, tab_ref, band):
    spec = dot(tab_ref[0], x, ((1,), (1,)))
    for term in range(1, tab_ref.shape[0]):
        spec = spec + dot(tab_ref[term], x, ((1,), (1,)))
    real, imag = spec[:BINS], spec[BINS:]
    amplitude = jnp.sqrt(real * real + imag * imag)
    high = amplitude.astype(BF16)
    low = (amplitude - high.astype(F32)).astype(BF16)
    near = dot(band, high, ((1,), (0,))) + dot(band, low, ((1,), (0,)))
    factor = live / (near * (1.0 / (2 * HALF_WIN + 1)) + 1e-06)
    real = (real * factor).reshape(PLANE, SLICE, LANES)
    imag = (imag * factor).reshape(PLANE, SLICE, LANES)
    return jnp.concatenate([real, imag], axis=1).astype(BF16)


def regroup(parts):
    group = lax.broadcasted_iota(jnp.int32, parts[0].shape, 1) // 32
    for bit in range(2):
        step = 32 << bit
        upper = (group // (1 << bit)) % 2 == 1
        new = list(parts)
        for i in range(4):
            if i & (1 << bit):
                continue
            a, b = parts[i], parts[i | (1 << bit)]
            new[i] = jnp.where(upper, pltpu.roll(b, step, 1), a)
            new[i | (1 << bit)] = jnp.where(upper, b, pltpu.roll(a, LANES - step, 1))
        parts = new
    return parts


def regroup_plane(ref, t_ref, plane):
    def take(s, _):
        from_z = lax.div(s, YC) * (Z_LO * YC) + lax.rem(s, YC)
        parts = regroup([ref[from_z + z * YC].astype(F32) for z in range(Z_LO)])
        for w in range(4):
            at = pl.ds(pl.multiple_of((s * 4 + w) * SLICE, SLICE), SLICE)
            t_ref[plane, 0, at] = parts[w][:SLICE]
            t_ref[plane, 1, at] = parts[w][SLICE:]
        return 0

    lax.fori_loop(0, 2 * YC, take, 0)


def stack_pairs(t_ref, u_ref):
    rows = lax.broadcasted_iota(jnp.int32, (LANES, LANES), 0)
    lanes = lax.broadcasted_iota(jnp.int32, (LANES, LANES), 1)
    for f in range(SLICE):
        every = pl.ds(f, WINS_ALL, stride=SLICE)
        a_re, a_im = t_ref[0, 0, every], t_ref[0, 1, every]
        own = jnp.concatenate([a_re, a_im], axis=0).astype(BF16)
        turned = jnp.concatenate([a_im, -a_re], axis=0).astype(BF16)
        further = jnp.concatenate([t_ref[1, 0, every], t_ref[1, 1, every]], axis=0).astype(BF16)
        both = jnp.concatenate([own, further], axis=1)
        for part, left in enumerate((own, turned)):
            pairs = dot(left, both, ((0,), (0,)))
            pairs = jnp.where(lanes > rows, pairs[:, :LANES], pairs[:, LANES:])
            u_ref[pl.ds(part * SLICE + f, LANES, stride=ROWS)] = pairs


def kernel(limit_ref, live_ref, x_hbm, tab_hbm, band_hbm, itab_hbm, out_ref,
           x_ref, tab_ref, band_ref, itab_ref, w_ref, near_ref, far_ref, t_ref, u_ref, s_ref, got_ref,
           local_sem, send_sem, near_sem, far_sem, got_sem):
    chan, win = lax.axis_index("chan"), lax.axis_index("win")
    x = lax.div(chan, Z_LO)
    z, yc = lax.div(win, YC) * Z_LO + lax.rem(chan, Z_LO), lax.rem(win, YC)
    me = z * YC + yc
    has_left, has_right = x > 0, x < X - 1

    def device(to_x, to_z, to_yc):
        return {"chan": to_x * Z_LO + lax.rem(to_z, Z_LO), "win": lax.div(to_z, Z_LO) * YC + to_yc}

    loads = [
        pltpu.make_async_copy(src, dst, local_sem.at[i])
        for i, (src, dst) in enumerate(
            ((x_hbm, x_ref), (tab_hbm, tab_ref), (band_hbm, band_ref), (itab_hbm, itab_ref)))
    ]
    for load in loads:
        load.start()

    barrier = pltpu.get_barrier_semaphore()

    def greet(i, _):
        peer = lax.rem(me + i, PLANE)
        to = device(x, lax.div(peer, YC), lax.rem(peer, YC))
        pl.semaphore_signal(barrier, inc=1, device_id=to, device_id_type=MESH)
        return 0

    lax.fori_loop(1, PLANE, greet, 0)

    @pl.when(has_right)
    def _():
        pl.semaphore_signal(barrier, inc=1, device_id=device(x + 1, z, yc), device_id_type=MESH)

    lane = lax.rem(lax.broadcasted_iota(jnp.int32, (1, LANES), 1), 32)
    live = jnp.zeros((1, LANES), F32)
    for c in range(32):
        live = jnp.where(lane == c, live_ref[c].astype(F32), live)
    for load in loads[:3]:
        load.wait()
    w_ref[...] = whiten(x_ref[...], live, tab_ref, band_ref[...])

    pl.semaphore_wait(barrier, PLANE - 1 + has_left.astype(jnp.int32))

    own = pltpu.make_async_copy(w_ref.at[me], near_ref.at[me], local_sem.at[4])
    own.start()
    order = (0, 4, 3, 5, 2, 6, 1, 7)

    for step in order:
        to_z = lax.rem(z + step, Z)

        def send(i, _, to_z=to_z):
            to_yc = lax.rem(yc + i, YC)
            pltpu.make_async_remote_copy(
                src_ref=w_ref.at[to_z * YC + to_yc], dst_ref=near_ref.at[me], send_sem=send_sem,
                recv_sem=near_sem.at[z], device_id=device(x, to_z, to_yc), device_id_type=MESH,
            ).start()
            return 0

        lax.fori_loop(0 if step else 1, YC, send, 0)

    @pl.when(jnp.logical_not(has_right))
    def _():
        far_ref[...] = jnp.zeros_like(far_ref)

    own.wait()
    for step in order:
        from_z = lax.rem(z + Z - step, Z)
        chunk = pl.ds(from_z * YC, YC)
        some = near_ref.at[pl.ds(0, YC if step else YC - 1)]
        pltpu.make_async_copy(some, some, near_sem.at[from_z]).wait()

        @pl.when(has_left)
        def _(chunk=chunk):
            pltpu.make_async_remote_copy(
                src_ref=near_ref.at[chunk], dst_ref=far_ref.at[chunk], send_sem=send_sem,
                recv_sem=far_sem, device_id=device(x - 1, z, yc), device_id_type=MESH,
            ).start()

    regroup_plane(near_ref, t_ref, 0)

    @pl.when(has_right)
    def _():
        pltpu.make_async_copy(far_ref, far_ref, far_sem).wait()

    regroup_plane(far_ref, t_ref, 1)
    stack_pairs(t_ref, u_ref)
    s_ref[...] = u_ref[...].astype(BF16).reshape(s_ref.shape)

    def owned(to_z, to_yc):
        return lax.rem(to_z, Z_LO) * (2 * YC) + lax.div(to_z, Z_LO) * YC + to_yc

    own = pltpu.make_async_copy(s_ref.at[owned(z, yc)], got_ref.at[me], local_sem.at[5])
    own.start()
    for step in order[1:] + order[:1]:
        to_z = lax.rem(z + step, Z)

        def give(i, _, to_z=to_z):
            to_yc = lax.rem(yc + i, YC)
            pltpu.make_async_remote_copy(
                src_ref=s_ref.at[owned(to_z, to_yc)], dst_ref=got_ref.at[me], send_sem=send_sem,
                recv_sem=got_sem, device_id=device(x, to_z, to_yc), device_id_type=MESH,
            ).start()
            return 0

        lax.fori_loop(0 if step else 1, YC, give, 0)

    own.wait()
    loads[3].wait()
    rest = got_ref.at[pl.ds(0, PLANE - 1)]
    pltpu.make_async_copy(rest, rest, got_sem).wait()

    right = jnp.concatenate([got_ref[:, c].reshape(SAMPLES, LANES) for c in range(2)], axis=1)
    pairs = dot(itab_ref[0], right, ((1,), (0,)))
    for term in range(1, itab_ref.shape[0]):
        pairs = pairs + dot(itab_ref[term], right, ((1,), (0,)))
    offsets = lax.broadcasted_iota(jnp.int32, (LAGS_PAD, LANES), 1) + 1
    first = lax.rem(chan, Z_LO) * 32 + win * 2
    for c in range(2):
        reach = jnp.minimum(limit_ref[win * 2 + c], CHANNELS - 1 - (chan * 32 + win * 2 + c))
        kept = pltpu.roll(pairs[:, c * LANES:(c + 1) * LANES], LANES - 1 - c - first, 1)
        out_ref[pl.ds(c, LAGS_PAD, stride=2)] = jnp.where(offsets <= reach, kept, 0.0)

    sent = w_ref.at[pl.ds(0, PLANE - 1)]
    pltpu.make_async_copy(sent, sent, send_sem).wait()
    pltpu.make_async_copy(rest, rest, send_sem).wait()

    @pl.when(has_left)
    def _():
        pltpu.make_async_copy(near_ref, near_ref, send_sem).wait()


def shards(records, live, band_limit):
    tab = jnp.asarray(forward_tables(2))
    band = jnp.asarray(band_table())
    itab = jnp.asarray(inverse_tables(2))
    rows = records.reshape(LANES, SAMPLES)
    smem, vmem, hbm = (pl.BlockSpec(memory_space=m) for m in (pltpu.SMEM, pltpu.VMEM, pl.ANY))
    out = pl.pallas_call(
        kernel,
        out_shape=jax.ShapeDtypeStruct((2 * LAGS_PAD, LANES), F32),
        in_specs=[smem, smem, hbm, hbm, hbm, hbm],
        out_specs=vmem,
        scratch_shapes=[
            pltpu.VMEM(rows.shape, BF16),
            pltpu.VMEM(tab.shape, BF16),
            pltpu.VMEM(band.shape, BF16),
            pltpu.VMEM(itab.shape, BF16),
            pltpu.VMEM((PLANE, ROWS, LANES), BF16),
            pltpu.VMEM((PLANE, ROWS, LANES), BF16),
            pltpu.VMEM((PLANE, ROWS, LANES), BF16),
            pltpu.VMEM((2, 2, WINS_ALL * SLICE, LANES), F32),
            pltpu.VMEM((LANES * ROWS, LANES), F32),
            pltpu.VMEM((PLANE, 2, ROWS, LANES), BF16),
            pltpu.VMEM((PLANE, 2, ROWS, LANES), BF16),
            pltpu.SemaphoreType.DMA((6,)),
            pltpu.SemaphoreType.DMA,
            pltpu.SemaphoreType.DMA((Z,)),
            pltpu.SemaphoreType.DMA,
            pltpu.SemaphoreType.DMA,
        ],
        compiler_params=pltpu.CompilerParams(
            collective_id=0, has_side_effects=True, vmem_limit_bytes=40 << 20
        ),
        cost_estimate=pl.CostEstimate(flops=1_500_000_000, bytes_accessed=8_000_000, transcendentals=65536),
        name="correlate",
    )(band_limit, live, rows, tab, band, itab)
    out = out.reshape(LAGS_PAD, 2, LANES)[:LAGS, :, :R]
    return jnp.transpose(out, (1, 2, 0))


def solution(mesh):
    placed = (P("win", "chan", None), P("chan"), P("chan"))
    return jax.shard_map(
        shards,
        mesh=mesh,
        in_specs=placed,
        out_specs=P(("chan", "win"), None, None),
        check_vma=False,
    )
```

```python
import math

import jax
import jax.numpy as jnp
import ml_dtypes
import numpy as np
from jax import lax
from jax.experimental import pallas as pl
from jax.experimental.pallas import tpu as pltpu
from jax.sharding import PartitionSpec as P

R = 100
HALF_LAG = 128
HALF_WIN = 32
SAMPLES = 1024
BINS = SAMPLES // 2
LAGS = 2 * HALF_LAG + 1
WINS_ALL = 64
CHANNELS = 512

LAGS_PAD = 272
X, Z_LO, Z, YC = 4, 4, 8, 8
PLANE = Z * YC
SLICE = BINS // PLANE
BLOCKS = 4
ROWS = 2 * SLICE
LANES = 128

MESH = pl.DeviceIdType.MESH
F32, BF16 = jnp.float32, jnp.bfloat16


def split(table, terms):
    parts, rest = [], table.astype(np.float64)
    for _ in range(terms):
        part = rest.astype(np.float32).astype(ml_dtypes.bfloat16)
        parts.append(part)
        rest = rest - part.astype(np.float64)
    return parts


RESIDUES = (0, 4, 1, 7, 2, 6, 3, 5)
RUN = BINS // 8
ORDER = np.concatenate([np.arange(RUN) * 8 + (r or 8) for r in RESIDUES])


def forward_tables(terms):
    groups = []
    for g in range(4):
        halves = []
        for side in range(2):
            freqs = ORDER[(2 * g + side) * RUN:(2 * g + side + 1) * RUN, None]
            phase = np.mod(freqs * np.arange(LANES)[None, :], SAMPLES) * (2.0 * math.pi / SAMPLES)
            cos, sin = np.cos(phase), np.sin(phase)
            if g == 0:
                real, imag = [np.zeros_like(cos)] * 2, [np.zeros_like(cos)] * 2
                real[side], imag[side] = cos, -sin
            else:
                sign = 1 - 2 * side
                real, imag = [cos, sign * sin], [-sin, sign * cos]
            halves.append((np.concatenate(real, axis=1), np.concatenate(imag, axis=1)))
        (real_a, imag_a), (real_b, imag_b) = halves
        groups.append(np.concatenate([real_a, real_b, imag_a, imag_b], axis=0))
    return np.stack(split(np.stack(groups), terms))


def inverse_tables(terms):
    freqs = ORDER[:, None]
    shifts = np.arange(LAGS)[None, :] - HALF_LAG
    phase = np.mod(freqs * shifts, SAMPLES) * (2.0 * math.pi / SAMPLES)
    factor = 2.0 / math.sqrt(SAMPLES * WINS_ALL)
    real = (np.cos(phase) * factor).reshape(PLANE, SLICE, LAGS)
    imag = (-np.sin(phase) * factor).reshape(PLANE, SLICE, LAGS)
    table = np.concatenate([real, imag], axis=1).reshape(SAMPLES, LAGS).T
    table = np.pad(table, ((0, LAGS_PAD - LAGS), (0, 0)))
    return np.stack(split(table, terms))


def band_table():
    return (np.abs(ORDER[:, None] - ORDER[None, :]) <= HALF_WIN).astype(ml_dtypes.bfloat16)


def dot(a, b, dims):
    return lax.dot_general(a, b, (dims, ((), ())), preferred_element_type=F32)


def residue_sums(x):
    b = [x[:, LANES * i:LANES * (i + 1)].astype(F32) for i in range(8)]
    plus = [b[i] + b[i + 4] for i in range(4)]
    minus = [b[i] - b[i + 4] for i in range(4)]
    even, odd = plus[0] + plus[2], plus[1] + plus[3]
    root = math.sqrt(0.5)
    across, along = (minus[1] - minus[3]) * root, (minus[1] + minus[3]) * root
    return (
        (even + odd, even - odd),
        (minus[0] + across, -minus[2] - along),
        (plus[0] - plus[2], plus[3] - plus[1]),
        (minus[0] - across, minus[2] - along),
    )


def whiten(x, live, tab_ref, band):
    real, imag = [], []
    for g, sums in enumerate(residue_sums(x)):
        sums = jnp.concatenate(sums, axis=1)
        high = sums.astype(BF16)
        low = (sums - high.astype(F32)).astype(BF16)
        spec = dot(tab_ref[0, g], high, ((1,), (1,)))
        spec = spec + dot(tab_ref[0, g], low, ((1,), (1,)))
        spec = spec + dot(tab_ref[1, g], high, ((1,), (1,)))
        real.append(spec[:2 * RUN])
        imag.append(spec[2 * RUN:])
    real, imag = jnp.concatenate(real, axis=0), jnp.concatenate(imag, axis=0)
    amplitude = jnp.sqrt(real * real + imag * imag)
    high = amplitude.astype(BF16)
    low = (amplitude - high.astype(F32)).astype(BF16)
    near = dot(band, high, ((1,), (0,))) + dot(band, low, ((1,), (0,)))
    factor = live / (near * (1.0 / (2 * HALF_WIN + 1)) + 1e-06)
    real = (real * factor).reshape(PLANE, SLICE, LANES)
    imag = (imag * factor).reshape(PLANE, SLICE, LANES)
    return jnp.concatenate([real, imag], axis=1).astype(BF16)


def regroup(parts):
    group = lax.broadcasted_iota(jnp.int32, parts[0].shape, 1) // 32
    for bit in range(2):
        step = 32 << bit
        upper = (group // (1 << bit)) % 2 == 1
        new = list(parts)
        for i in range(4):
            if i & (1 << bit):
                continue
            a, b = parts[i], parts[i | (1 << bit)]
            new[i] = jnp.where(upper, pltpu.roll(b, step, 1), a)
            new[i | (1 << bit)] = jnp.where(upper, b, pltpu.roll(a, LANES - step, 1))
        parts = new
    return parts


def regroup_plane(ref, t_ref, plane):
    def take(s, _):
        from_z = lax.div(s, YC) * (Z_LO * YC) + lax.rem(s, YC)
        parts = regroup([ref[from_z + z * YC].astype(F32) for z in range(Z_LO)])
        for w in range(4):
            at = pl.ds(pl.multiple_of((s * 4 + w) * SLICE, SLICE), SLICE)
            t_ref[plane, 0, at] = parts[w][:SLICE]
            t_ref[plane, 1, at] = parts[w][SLICE:]
        return 0

    lax.fori_loop(0, 2 * YC, take, 0)


def columns(t_ref, plane, f):
    every = pl.ds(f, WINS_ALL, stride=SLICE)
    re, im = t_ref[plane, 0, every], t_ref[plane, 1, every]
    own = jnp.concatenate([re, im], axis=0)
    turned = jnp.concatenate([-im, re], axis=0)
    return own, jnp.concatenate([own, turned], axis=1).astype(BF16)


def near_pairs(t_ref, u_ref, left_ref):
    for f in range(SLICE):
        own, both = columns(t_ref, 0, f)
        left = own.T.astype(BF16)
        left_ref[f] = left
        pairs = dot(left, both, ((1,), (0,)))
        for part in range(2):
            u_ref[pl.ds(part * SLICE + f, LANES, stride=ROWS)] = pairs[:, part * LANES:(part + 1) * LANES]


def far_pairs(t_ref, u_ref, left_ref, both_ref, s_ref, block):
    size = LANES // BLOCKS
    rows = lax.broadcasted_iota(jnp.int32, (size, LANES), 0) + block * size
    near = lax.broadcasted_iota(jnp.int32, (size, LANES), 1) > rows
    for f in range(SLICE):
        if block == 0:
            both_ref[f] = columns(t_ref, 1, f)[1]
        pairs = dot(left_ref[f, block * size:(block + 1) * size], both_ref[f], ((1,), (0,)))
        for part in range(2):
            at = pl.ds(block * size * ROWS + part * SLICE + f, size, stride=ROWS)
            u_ref[at] = jnp.where(near, u_ref[at], pairs[:, part * LANES:(part + 1) * LANES])
    done = u_ref[block * size * ROWS:(block + 1) * size * ROWS]
    s_ref[block * size // 2:(block + 1) * size // 2] = done.astype(BF16).reshape(size // 2, 2, ROWS, LANES)


def kernel(limit_hbm, live_hbm, x_hbm, tab_hbm, band_hbm, itab_hbm, out_ref,
           limit_ref, live_ref, x_ref, tab_ref, band_ref, itab_ref, w_ref, near_ref, far_ref, t_ref, u_ref, left_ref, both_ref, s_ref, got_ref,
           local_sem, send_sem, near_sem, far_sem, got_sem, ready_sem):
    chan, win = lax.axis_index("chan"), lax.axis_index("win")
    x = lax.div(chan, Z_LO)
    z, yc = lax.div(win, YC) * Z_LO + lax.rem(chan, Z_LO), lax.rem(win, YC)
    me = z * YC + yc
    has_left, has_right = x > 0, x < X - 1

    def device(to_x, to_z, to_yc):
        return {"chan": to_x * Z_LO + lax.rem(to_z, Z_LO), "win": lax.div(to_z, Z_LO) * YC + to_yc}

    loads = [
        pltpu.make_async_copy(src, dst, local_sem.at[i])
        for i, (src, dst) in enumerate(
            ((live_hbm, live_ref), (x_hbm, x_ref), (tab_hbm, tab_ref), (band_hbm, band_ref),
             (itab_hbm, itab_ref), (limit_hbm, limit_ref)))
    ]
    for load in loads[:4]:
        load.start()

    barrier = pltpu.get_barrier_semaphore()

    def signal(semaphore, to):
        pl.semaphore_signal(semaphore, inc=1, device_id=to, device_id_type=MESH)

    for step in range(1, Z):
        signal(barrier, device(x, lax.rem(z + step, Z), yc))
    for step in range(1, YC):
        signal(barrier, device(x, z, lax.rem(yc + step, YC)))

    @pl.when(has_right)
    def _():
        signal(barrier, device(x + 1, z, yc))

    for load in loads[4:]:
        load.start()
    lane = lax.rem(lax.broadcasted_iota(jnp.int32, (1, LANES), 1), 32)
    live = jnp.zeros((1, LANES), F32)
    loads[0].wait()
    for c in range(32):
        live = jnp.where(lane == c, live_ref[c].astype(F32), live)
    for load in loads[1:4]:
        load.wait()
    w_ref[...] = whiten(x_ref[...], live, tab_ref, band_ref[...])

    pl.semaphore_wait(barrier, Z - 1 + YC - 1 + has_left.astype(jnp.int32))
    for step in range(1, YC):
        signal(ready_sem, device(x, z, lax.rem(yc + step, YC)))

    own = pltpu.make_async_copy(w_ref.at[me], near_ref.at[me], local_sem.at[6])
    own.start()
    order = (0, 1, 7, 2, 6, 3, 5, 4)

    def send(to_z, to_yc):
        pltpu.make_async_remote_copy(
            src_ref=w_ref.at[to_z * YC + to_yc], dst_ref=near_ref.at[me], send_sem=send_sem,
            recv_sem=near_sem.at[z], device_id=device(x, to_z, to_yc), device_id_type=MESH,
        ).start()

    for step in order[1:]:
        send(lax.rem(z + step, Z), yc)
    for step in range(1, YC):
        send(z, lax.rem(yc + step, YC))
    pl.semaphore_wait(ready_sem, YC - 1)
    for step in order[1:]:
        to_z = lax.rem(z + step, Z)

        def send_on(i, _, to_z=to_z):
            send(to_z, lax.rem(yc + i, YC))
            return 0

        lax.fori_loop(1, YC, send_on, 0)

    @pl.when(jnp.logical_not(has_right))
    def _():
        far_ref[...] = jnp.zeros_like(far_ref)

    own.wait()
    for step in order:
        from_z = lax.rem(z + Z - step, Z)
        chunk = pl.ds(from_z * YC, YC)
        some = near_ref.at[pl.ds(0, YC if step else YC - 1)]
        pltpu.make_async_copy(some, some, near_sem.at[from_z]).wait()

        @pl.when(has_left)
        def _(chunk=chunk):
            pltpu.make_async_remote_copy(
                src_ref=near_ref.at[chunk], dst_ref=far_ref.at[chunk], send_sem=send_sem,
                recv_sem=far_sem, device_id=device(x - 1, z, yc), device_id_type=MESH,
            ).start()

    regroup_plane(near_ref, t_ref, 0)
    near_pairs(t_ref, u_ref, left_ref)

    @pl.when(has_right)
    def _():
        pltpu.make_async_copy(far_ref, far_ref, far_sem).wait()

    regroup_plane(far_ref, t_ref, 1)

    def owned(to_z, to_yc):
        return lax.rem(to_z, Z_LO) * (2 * YC) + lax.div(to_z, Z_LO) * YC + to_yc

    own = pltpu.make_async_copy(s_ref.at[owned(z, yc)], got_ref.at[me], local_sem.at[7])
    for block in range(BLOCKS):
        far_pairs(t_ref, u_ref, left_ref, both_ref, s_ref, block)

        def give(i, _, block=block):
            to_yc = lax.rem(yc + i, YC)
            for low in range(block * Z_LO // BLOCKS, (block + 1) * Z_LO // BLOCKS):
                for high in range(2):
                    to_z = high * Z_LO + low

                    @pl.when(to_z * YC + to_yc != me)
                    def _(to_z=to_z):
                        pltpu.make_async_remote_copy(
                            src_ref=s_ref.at[owned(to_z, to_yc)], dst_ref=got_ref.at[me], send_sem=send_sem,
                            recv_sem=got_sem, device_id=device(x, to_z, to_yc), device_id_type=MESH,
                        ).start()
            return 0

        lax.fori_loop(0, YC, give, 0)

    own.start()
    own.wait()
    loads[4].wait()
    loads[5].wait()
    rest = got_ref.at[pl.ds(0, PLANE - 1)]
    pltpu.make_async_copy(rest, rest, got_sem).wait()

    right = jnp.concatenate([got_ref[:, c].reshape(SAMPLES, LANES) for c in range(2)], axis=1)
    pairs = dot(itab_ref[0], right, ((1,), (0,)))
    for term in range(1, itab_ref.shape[0]):
        pairs = pairs + dot(itab_ref[term], right, ((1,), (0,)))
    offsets = lax.broadcasted_iota(jnp.int32, (LAGS_PAD, LANES), 1) + 1
    first = lax.rem(chan, Z_LO) * 32 + win * 2
    for c in range(2):
        reach = jnp.minimum(limit_ref[win * 2 + c], CHANNELS - 1 - (chan * 32 + win * 2 + c))
        kept = pltpu.roll(pairs[:, c * LANES:(c + 1) * LANES], LANES - 1 - c - first, 1)
        out_ref[pl.ds(c, LAGS_PAD, stride=2)] = jnp.where(offsets <= reach, kept, 0.0)

    sent = w_ref.at[pl.ds(0, PLANE - 1)]
    pltpu.make_async_copy(sent, sent, send_sem).wait()
    pltpu.make_async_copy(rest, rest, send_sem).wait()

    @pl.when(has_left)
    def _():
        pltpu.make_async_copy(near_ref, near_ref, send_sem).wait()


def shards(records, live, band_limit):
    tab = jnp.asarray(forward_tables(2))
    band = jnp.asarray(band_table())
    itab = jnp.asarray(inverse_tables(2))
    rows = records.reshape(LANES, SAMPLES)
    vmem, hbm = pl.BlockSpec(memory_space=pltpu.VMEM), pl.BlockSpec(memory_space=pltpu.HBM)
    out = pl.pallas_call(
        kernel,
        out_shape=jax.ShapeDtypeStruct((2 * LAGS_PAD, LANES), F32),
        in_specs=[hbm] * 6,
        out_specs=vmem,
        scratch_shapes=[
            pltpu.SMEM(band_limit.shape, jnp.int32),
            pltpu.SMEM(live.shape, jnp.int32),
            pltpu.VMEM(rows.shape, BF16),
            pltpu.VMEM(tab.shape, BF16),
            pltpu.VMEM(band.shape, BF16),
            pltpu.VMEM(itab.shape, BF16),
            pltpu.VMEM((PLANE, ROWS, LANES), BF16),
            pltpu.VMEM((PLANE, ROWS, LANES), BF16),
            pltpu.VMEM((PLANE, ROWS, LANES), BF16),
            pltpu.VMEM((2, 2, WINS_ALL * SLICE, LANES), F32),
            pltpu.VMEM((LANES * ROWS, LANES), F32),
            pltpu.VMEM((SLICE, LANES, LANES), BF16),
            pltpu.VMEM((SLICE, LANES, 2 * LANES), BF16),
            pltpu.VMEM((PLANE, 2, ROWS, LANES), BF16),
            pltpu.VMEM((PLANE, 2, ROWS, LANES), BF16),
            pltpu.SemaphoreType.DMA((8,)),
            pltpu.SemaphoreType.DMA,
            pltpu.SemaphoreType.DMA((Z,)),
            pltpu.SemaphoreType.DMA,
            pltpu.SemaphoreType.DMA,
            pltpu.SemaphoreType.REGULAR,
        ],
        compiler_params=pltpu.CompilerParams(
            collective_id=0, has_side_effects=True, vmem_limit_bytes=40 << 20
        ),
        cost_estimate=pl.CostEstimate(flops=1_500_000_000, bytes_accessed=8_000_000, transcendentals=65536),
        name="correlate",
    )(*[pltpu.with_memory_space_constraint(a, pltpu.HBM) for a in (band_limit, live, rows, tab, band, itab)])
    out = out.reshape(LAGS_PAD, 2, LANES)[:LAGS, :, :R]
    return jnp.transpose(out, (1, 2, 0))


def solution(mesh):
    placed = (P("win", "chan", None), P("chan"), P("chan"))
    return jax.shard_map(
        shards,
        mesh=mesh,
        in_specs=placed,
        out_specs=P(("chan", "win"), None, None),
        check_vma=False,
    )
```

```python
import math

import jax
import jax.numpy as jnp
import ml_dtypes
import numpy as np
from jax import lax
from jax.experimental import pallas as pl
from jax.experimental.pallas import tpu as pltpu
from jax.sharding import PartitionSpec as P

R = 100
LANES = 128
HALF_LAG = 128
HALF_WIN = 32
SAMPLES = 1024
BINS = SAMPLES // 2
LAGS = 2 * HALF_LAG + 1
WINS_ALL = 64
CHANNELS = 512

LAGS_PAD = 272
X, Z_LO, Z, YC = 4, 4, 8, 8
PLANE = Z * YC
SLICE = BINS // PLANE
EARLY = (LANES - R) // 4 * 4
BLOCKS = ((16, EARLY, 64), (64, 64, 96), (96, 96, 128))
ROWS = 2 * SLICE

MESH = pl.DeviceIdType.MESH
F32, BF16 = jnp.float32, jnp.bfloat16


def split(table, terms):
    parts, rest = [], table.astype(np.float64)
    for _ in range(terms):
        part = rest.astype(np.float32).astype(ml_dtypes.bfloat16)
        parts.append(part)
        rest = rest - part.astype(np.float64)
    return parts


RESIDUES = (0, 4, 1, 7, 2, 6, 3, 5)
RUN = BINS // 8
ORDER = np.concatenate([np.arange(RUN) * 8 + (r or 8) for r in RESIDUES])


def forward_tables(terms):
    groups = []
    for g in range(4):
        halves = []
        for side in range(2):
            freqs = ORDER[(2 * g + side) * RUN:(2 * g + side + 1) * RUN, None]
            phase = np.mod(freqs * np.arange(LANES)[None, :], SAMPLES) * (2.0 * math.pi / SAMPLES)
            cos, sin = np.cos(phase), np.sin(phase)
            if g == 0:
                real, imag = [np.zeros_like(cos)] * 2, [np.zeros_like(cos)] * 2
                real[side], imag[side] = cos, -sin
            else:
                sign = 1 - 2 * side
                real, imag = [cos, sign * sin], [-sin, sign * cos]
            halves.append((np.concatenate(real, axis=1), np.concatenate(imag, axis=1)))
        (real_a, imag_a), (real_b, imag_b) = halves
        groups.append(np.concatenate([real_a, real_b, imag_a, imag_b], axis=0))
    return np.stack(split(np.stack(groups), terms))


def inverse_tables(terms):
    freqs = ORDER[:, None]
    shifts = np.arange(LAGS)[None, :] - HALF_LAG
    phase = np.mod(freqs * shifts, SAMPLES) * (2.0 * math.pi / SAMPLES)
    factor = 2.0 / math.sqrt(SAMPLES * WINS_ALL)
    real = (np.cos(phase) * factor).reshape(PLANE, SLICE, LAGS)
    imag = (-np.sin(phase) * factor).reshape(PLANE, SLICE, LAGS)
    table = np.concatenate([real, imag], axis=1).reshape(SAMPLES, LAGS).T
    table = np.pad(table, ((0, LAGS_PAD - LAGS), (0, 0)))
    return np.stack(split(table, terms))


def band_table():
    return (np.abs(ORDER[:, None] - ORDER[None, :]) <= HALF_WIN).astype(ml_dtypes.bfloat16)


def dot(a, b, dims):
    return lax.dot_general(a, b, (dims, ((), ())), preferred_element_type=F32)


def residue_sums(x):
    b = [x[:, LANES * i:LANES * (i + 1)].astype(F32) for i in range(8)]
    plus = [b[i] + b[i + 4] for i in range(4)]
    minus = [b[i] - b[i + 4] for i in range(4)]
    even, odd = plus[0] + plus[2], plus[1] + plus[3]
    root = math.sqrt(0.5)
    across, along = (minus[1] - minus[3]) * root, (minus[1] + minus[3]) * root
    return (
        (even + odd, even - odd),
        (minus[0] + across, -minus[2] - along),
        (plus[0] - plus[2], plus[3] - plus[1]),
        (minus[0] - across, minus[2] - along),
    )


def whiten(x, live, tab_ref, band):
    real, imag = [], []
    for g, sums in enumerate(residue_sums(x)):
        sums = jnp.concatenate(sums, axis=1)
        high = sums.astype(BF16)
        low = (sums - high.astype(F32)).astype(BF16)
        spec = dot(tab_ref[0, g], high, ((1,), (1,)))
        spec = spec + dot(tab_ref[0, g], low, ((1,), (1,)))
        spec = spec + dot(tab_ref[1, g], high, ((1,), (1,)))
        real.append(spec[:2 * RUN])
        imag.append(spec[2 * RUN:])
    real, imag = jnp.concatenate(real, axis=0), jnp.concatenate(imag, axis=0)
    amplitude = jnp.sqrt(real * real + imag * imag)
    high = amplitude.astype(BF16)
    low = (amplitude - high.astype(F32)).astype(BF16)
    near = dot(band, high, ((1,), (0,))) + dot(band, low, ((1,), (0,)))
    factor = live / (near * (1.0 / (2 * HALF_WIN + 1)) + 1e-06)
    real = (real * factor).reshape(PLANE, SLICE, LANES)
    imag = (imag * factor).reshape(PLANE, SLICE, LANES)
    return jnp.concatenate([real, imag], axis=1).astype(BF16)


def regroup(parts):
    group = lax.broadcasted_iota(jnp.int32, parts[0].shape, 1) // 32
    for bit in range(2):
        step = 32 << bit
        upper = (group // (1 << bit)) % 2 == 1
        new = list(parts)
        for i in range(4):
            if i & (1 << bit):
                continue
            a, b = parts[i], parts[i | (1 << bit)]
            new[i] = jnp.where(upper, pltpu.roll(b, step, 1), a)
            new[i | (1 << bit)] = jnp.where(upper, b, pltpu.roll(a, LANES - step, 1))
        parts = new
    return parts


def regroup_plane(ref, t_ref, plane):
    def take(s, _):
        from_z = lax.div(s, YC) * (Z_LO * YC) + lax.rem(s, YC)
        parts = regroup([ref[from_z + z * YC].astype(F32) for z in range(Z_LO)])
        for w in range(4):
            at = pl.ds(pl.multiple_of((s * 4 + w) * SLICE, SLICE), SLICE)
            t_ref[plane, 0, at] = parts[w][:SLICE]
            t_ref[plane, 1, at] = parts[w][SLICE:]
        return 0

    lax.fori_loop(0, 2 * YC, take, 0, unroll=16)


def columns(t_ref, plane, f):
    every = pl.ds(f, WINS_ALL, stride=SLICE)
    re, im = t_ref[plane, 0, every], t_ref[plane, 1, every]
    own = jnp.concatenate([re, im], axis=0)
    turned = jnp.concatenate([-im, re], axis=0)
    return own, jnp.concatenate([own, turned], axis=1).astype(BF16)


def near_pairs(t_ref, u_ref, left_ref):
    for f in range(SLICE):
        own, both = columns(t_ref, 0, f)
        left = own.T.astype(BF16)
        left_ref[f] = left
        pairs = dot(left, both, ((1,), (0,)))
        for part in range(2):
            u_ref[pl.ds(part * SLICE + f, LANES, stride=ROWS)] = pairs[:, part * LANES:(part + 1) * LANES]


def far_pairs(t_ref, u_ref, left_ref, both_ref, start, end, first):
    rows = lax.broadcasted_iota(jnp.int32, (end - start, LANES), 0) + start
    near = lax.broadcasted_iota(jnp.int32, (end - start, LANES), 1) > rows
    for f in range(SLICE):
        if first:
            both_ref[f] = columns(t_ref, 1, f)[1]
        pairs = dot(left_ref[f, start:end], both_ref[f], ((1,), (0,)))
        for part in range(2):
            at = pl.ds(start * ROWS + part * SLICE + f, end - start, stride=ROWS)
            u_ref[at] = jnp.where(near, u_ref[at], pairs[:, part * LANES:(part + 1) * LANES])


def round_rows(u_ref, s_ref, start, end):
    done = u_ref[start * ROWS:end * ROWS]
    s_ref[start // 2:end // 2] = done.astype(BF16).reshape((end - start) // 2, 2, ROWS, LANES)


def kernel(limit_hbm, live_hbm, x_hbm, tab_hbm, band_hbm, itab_hbm, out_ref,
           limit_ref, live_ref, x_ref, tab_ref, band_ref, itab_ref, w_ref, near_ref, far_ref, t_ref, u_ref, left_ref, both_ref, s_ref, got_ref,
           local_sem, send_sem, near_sem, far_sem, got_sem, ready_sem):
    chan, win = lax.axis_index("chan"), lax.axis_index("win")
    x = lax.div(chan, Z_LO)
    z, yc = lax.div(win, YC) * Z_LO + lax.rem(chan, Z_LO), lax.rem(win, YC)
    me = z * YC + yc
    has_left, has_right = x > 0, x < X - 1

    def device(to_x, to_z, to_yc):
        return {"chan": to_x * Z_LO + lax.rem(to_z, Z_LO), "win": lax.div(to_z, Z_LO) * YC + to_yc}

    loads = [
        pltpu.make_async_copy(src, dst, local_sem.at[i])
        for i, (src, dst) in enumerate(
            ((live_hbm, live_ref), (x_hbm, x_ref), (tab_hbm, tab_ref), (band_hbm, band_ref),
             (itab_hbm, itab_ref), (limit_hbm, limit_ref)))
    ]
    for load in loads[:4]:
        load.start()

    barrier = pltpu.get_barrier_semaphore()

    def signal(semaphore, to):
        pl.semaphore_signal(semaphore, inc=1, device_id=to, device_id_type=MESH)

    for step in range(1, Z):
        signal(barrier, device(x, lax.rem(z + step, Z), yc))
    for step in range(1, YC):
        signal(barrier, device(x, z, lax.rem(yc + step, YC)))

    @pl.when(has_right)
    def _():
        signal(barrier, device(x + 1, z, yc))

    for load in loads[4:]:
        load.start()
    lane = lax.rem(lax.broadcasted_iota(jnp.int32, (1, LANES), 1), 32)
    live = jnp.zeros((1, LANES), F32)
    loads[0].wait()
    for c in range(32):
        live = jnp.where(lane == c, live_ref[c].astype(F32), live)
    for load in loads[1:4]:
        load.wait()
    w_ref[...] = whiten(x_ref[...], live, tab_ref, band_ref[...])

    pl.semaphore_wait(barrier, Z - 1 + YC - 1 + has_left.astype(jnp.int32))
    for step in range(1, YC):
        signal(ready_sem, device(x, z, lax.rem(yc + step, YC)))

    own = pltpu.make_async_copy(w_ref.at[me], near_ref.at[me], local_sem.at[6])
    own.start()
    order = (0, 1, 7, 2, 6, 3, 5, 4)

    def send(to_z, to_yc):
        pltpu.make_async_remote_copy(
            src_ref=w_ref.at[to_z * YC + to_yc], dst_ref=near_ref.at[me], send_sem=send_sem,
            recv_sem=near_sem.at[z], device_id=device(x, to_z, to_yc), device_id_type=MESH,
        ).start()

    for step in order[1:]:
        send(lax.rem(z + step, Z), yc)
    for step in range(1, YC):
        send(z, lax.rem(yc + step, YC))
    pl.semaphore_wait(ready_sem, YC - 1)
    for step in order[1:]:
        to_z = lax.rem(z + step, Z)

        def send_on(i, _, to_z=to_z):
            send(to_z, lax.rem(yc + i, YC))
            return 0

        lax.fori_loop(1, YC, send_on, 0)

    @pl.when(jnp.logical_not(has_right))
    def _():
        far_ref[...] = jnp.zeros_like(far_ref)

    own.wait()
    for step in order:
        from_z = lax.rem(z + Z - step, Z)
        chunk = pl.ds(from_z * YC, YC)
        some = near_ref.at[pl.ds(0, YC if step else YC - 1)]
        pltpu.make_async_copy(some, some, near_sem.at[from_z]).wait()

        @pl.when(has_left)
        def _(chunk=chunk):
            pltpu.make_async_remote_copy(
                src_ref=near_ref.at[chunk], dst_ref=far_ref.at[chunk], send_sem=send_sem,
                recv_sem=far_sem, device_id=device(x - 1, z, yc), device_id_type=MESH,
            ).start()

    def give(start, end):
        round_rows(u_ref, s_ref, start, end)
        first, count = start // 2, (end - start) // 2

        def go(i, _):
            pair = first + lax.rem(i + z * 2 + yc, count)
            to_z = lax.div(lax.rem(pair, 2 * YC), YC) * Z_LO + lax.div(pair, 2 * YC)
            to_yc = lax.rem(pair, YC)

            @pl.when(to_z * YC + to_yc != me)
            def _():
                pltpu.make_async_remote_copy(
                    src_ref=s_ref.at[pair], dst_ref=got_ref.at[me], send_sem=send_sem,
                    recv_sem=got_sem, device_id=device(x, to_z, to_yc), device_id_type=MESH,
                ).start()
            return 0

        lax.fori_loop(0, count, go, 0)

    regroup_plane(near_ref, t_ref, 0)
    near_pairs(t_ref, u_ref, left_ref)
    give(0, EARLY)

    @pl.when(has_right)
    def _():
        pltpu.make_async_copy(far_ref, far_ref, far_sem).wait()

    regroup_plane(far_ref, t_ref, 1)
    for start, send_start, end in BLOCKS:
        far_pairs(t_ref, u_ref, left_ref, both_ref, start, end, start == BLOCKS[0][0])
        give(send_start, end)

    owned = lax.rem(z, Z_LO) * (2 * YC) + lax.div(z, Z_LO) * YC + yc
    own = pltpu.make_async_copy(s_ref.at[owned], got_ref.at[me], local_sem.at[7])
    own.start()
    own.wait()
    loads[4].wait()
    loads[5].wait()
    rest = got_ref.at[pl.ds(0, PLANE - 1)]
    pltpu.make_async_copy(rest, rest, got_sem).wait()

    right = jnp.concatenate([got_ref[:, c].reshape(SAMPLES, LANES) for c in range(2)], axis=1)
    pairs = dot(itab_ref[0], right, ((1,), (0,)))
    for term in range(1, itab_ref.shape[0]):
        pairs = pairs + dot(itab_ref[term], right, ((1,), (0,)))
    offsets = lax.broadcasted_iota(jnp.int32, (LAGS_PAD, LANES), 1) + 1
    first = lax.rem(chan, Z_LO) * 32 + win * 2
    for c in range(2):
        reach = jnp.minimum(limit_ref[win * 2 + c], CHANNELS - 1 - (chan * 32 + win * 2 + c))
        kept = pltpu.roll(pairs[:, c * LANES:(c + 1) * LANES], LANES - 1 - c - first, 1)
        out_ref[pl.ds(c, LAGS_PAD, stride=2)] = jnp.where(offsets <= reach, kept, 0.0)

    sent = w_ref.at[pl.ds(0, PLANE - 1)]
    pltpu.make_async_copy(sent, sent, send_sem).wait()
    pltpu.make_async_copy(rest, rest, send_sem).wait()

    @pl.when(has_left)
    def _():
        pltpu.make_async_copy(near_ref, near_ref, send_sem).wait()


def shards(records, live, band_limit):
    tab = jnp.asarray(forward_tables(2))
    band = jnp.asarray(band_table())
    itab = jnp.asarray(inverse_tables(2))
    rows = records.reshape(LANES, SAMPLES)
    vmem, hbm = pl.BlockSpec(memory_space=pltpu.VMEM), pl.BlockSpec(memory_space=pltpu.HBM)
    out = pl.pallas_call(
        kernel,
        out_shape=jax.ShapeDtypeStruct((2 * LAGS_PAD, LANES), F32),
        in_specs=[hbm] * 6,
        out_specs=vmem,
        scratch_shapes=[
            pltpu.SMEM(band_limit.shape, jnp.int32),
            pltpu.SMEM(live.shape, jnp.int32),
            pltpu.VMEM(rows.shape, BF16),
            pltpu.VMEM(tab.shape, BF16),
            pltpu.VMEM(band.shape, BF16),
            pltpu.VMEM(itab.shape, BF16),
            pltpu.VMEM((PLANE, ROWS, LANES), BF16),
            pltpu.VMEM((PLANE, ROWS, LANES), BF16),
            pltpu.VMEM((PLANE, ROWS, LANES), BF16),
            pltpu.VMEM((2, 2, WINS_ALL * SLICE, LANES), F32),
            pltpu.VMEM((LANES * ROWS, LANES), F32),
            pltpu.VMEM((SLICE, LANES, LANES), BF16),
            pltpu.VMEM((SLICE, LANES, 2 * LANES), BF16),
            pltpu.VMEM((PLANE, 2, ROWS, LANES), BF16),
            pltpu.VMEM((PLANE, 2, ROWS, LANES), BF16),
            pltpu.SemaphoreType.DMA((8,)),
            pltpu.SemaphoreType.DMA,
            pltpu.SemaphoreType.DMA((Z,)),
            pltpu.SemaphoreType.DMA,
            pltpu.SemaphoreType.DMA,
            pltpu.SemaphoreType.REGULAR,
        ],
        compiler_params=pltpu.CompilerParams(
            collective_id=0, has_side_effects=True, vmem_limit_bytes=40 << 20
        ),
        cost_estimate=pl.CostEstimate(flops=1_500_000_000, bytes_accessed=8_000_000, transcendentals=65536),
        name="correlate",
    )(*[pltpu.with_memory_space_constraint(a, pltpu.HBM) for a in (band_limit, live, rows, tab, band, itab)])
    out = out.reshape(LAGS_PAD, 2, LANES)[:LAGS, :, :R]
    return jnp.transpose(out, (1, 2, 0))


def solution(mesh):
    placed = (P("win", "chan", None), P("chan"), P("chan"))
    return jax.shard_map(
        shards,
        mesh=mesh,
        in_specs=placed,
        out_specs=P(("chan", "win"), None, None),
        check_vma=False,
    )
```

```python
import math

import jax
import jax.numpy as jnp
import ml_dtypes
import numpy as np
from jax import lax
from jax.experimental import pallas as pl
from jax.experimental.pallas import tpu as pltpu
from jax.sharding import PartitionSpec as P

R = 100
LANES = 128
HALF_LAG = 128
HALF_WIN = 32
SAMPLES = 1024
BINS = SAMPLES // 2
LAGS = 2 * HALF_LAG + 1
WINS_ALL = 64
CHANNELS = 512

LAGS_PAD = 272
X, Z_LO, Z, YC = 4, 4, 8, 8
PLANE = Z * YC
SLICE = BINS // PLANE
EARLY = (LANES - R) // 4 * 4
BLOCKS = ((16, EARLY, 64), (64, 64, 96), (96, 96, 128))
ROWS = 2 * SLICE
REST = R - (Z_LO - 1) * 32

MESH = pl.DeviceIdType.MESH
F32, BF16 = jnp.float32, jnp.bfloat16


def split(table, terms):
    parts, rest = [], table.astype(np.float64)
    for _ in range(terms):
        part = rest.astype(np.float32).astype(ml_dtypes.bfloat16)
        parts.append(part)
        rest = rest - part.astype(np.float64)
    return parts


RESIDUES = (0, 4, 1, 7, 2, 6, 3, 5)
RUN = BINS // 8
ORDER = np.concatenate([np.arange(RUN) * 8 + (r or 8) for r in RESIDUES])


def forward_tables(terms):
    groups = []
    for g in range(4):
        halves = []
        for side in range(2):
            freqs = ORDER[(2 * g + side) * RUN:(2 * g + side + 1) * RUN, None]
            phase = np.mod(freqs * np.arange(LANES)[None, :], SAMPLES) * (2.0 * math.pi / SAMPLES)
            cos, sin = np.cos(phase), np.sin(phase)
            if g == 0:
                real, imag = [np.zeros_like(cos)] * 2, [np.zeros_like(cos)] * 2
                real[side], imag[side] = cos, -sin
            else:
                sign = 1 - 2 * side
                real, imag = [cos, sign * sin], [-sin, sign * cos]
            halves.append((np.concatenate(real, axis=1), np.concatenate(imag, axis=1)))
        (real_a, imag_a), (real_b, imag_b) = halves
        groups.append(np.concatenate([real_a, real_b, imag_a, imag_b], axis=0))
    return np.stack(split(np.stack(groups), terms))


def inverse_tables(terms):
    freqs = ORDER[:, None]
    shifts = np.arange(LAGS)[None, :] - HALF_LAG
    phase = np.mod(freqs * shifts, SAMPLES) * (2.0 * math.pi / SAMPLES)
    factor = 2.0 / math.sqrt(SAMPLES * WINS_ALL)
    real = (np.cos(phase) * factor).reshape(PLANE, SLICE, LAGS)
    imag = (-np.sin(phase) * factor).reshape(PLANE, SLICE, LAGS)
    table = np.concatenate([real, imag], axis=1).reshape(SAMPLES, LAGS).T
    table = np.pad(table, ((0, LAGS_PAD - LAGS), (0, 0)))
    return np.stack(split(table, terms))


def band_table():
    return (np.abs(ORDER[:, None] - ORDER[None, :]) <= HALF_WIN).astype(ml_dtypes.bfloat16)


def dot(a, b, dims):
    return lax.dot_general(a, b, (dims, ((), ())), preferred_element_type=F32)


def residue_sums(x):
    b = [x[:, LANES * i:LANES * (i + 1)].astype(F32) for i in range(8)]
    plus = [b[i] + b[i + 4] for i in range(4)]
    minus = [b[i] - b[i + 4] for i in range(4)]
    even, odd = plus[0] + plus[2], plus[1] + plus[3]
    root = math.sqrt(0.5)
    across, along = (minus[1] - minus[3]) * root, (minus[1] + minus[3]) * root
    return (
        (even + odd, even - odd),
        (minus[0] + across, -minus[2] - along),
        (plus[0] - plus[2], plus[3] - plus[1]),
        (minus[0] - across, minus[2] - along),
    )


def whiten(x, live, tab_ref, band):
    real, imag = [], []
    for g, sums in enumerate(residue_sums(x)):
        sums = jnp.concatenate(sums, axis=1)
        high = sums.astype(BF16)
        low = (sums - high.astype(F32)).astype(BF16)
        spec = dot(tab_ref[0, g], high, ((1,), (1,)))
        spec = spec + dot(tab_ref[0, g], low, ((1,), (1,)))
        spec = spec + dot(tab_ref[1, g], high, ((1,), (1,)))
        real.append(spec[:2 * RUN])
        imag.append(spec[2 * RUN:])
    real, imag = jnp.concatenate(real, axis=0), jnp.concatenate(imag, axis=0)
    amplitude = jnp.sqrt(real * real + imag * imag)
    high = amplitude.astype(BF16)
    low = (amplitude - high.astype(F32)).astype(BF16)
    near = dot(band, high, ((1,), (0,))) + dot(band, low, ((1,), (0,)))
    factor = live / (near * (1.0 / (2 * HALF_WIN + 1)) + 1e-06)
    real = (real * factor).reshape(PLANE, SLICE, LANES)
    imag = (imag * factor).reshape(PLANE, SLICE, LANES)
    return jnp.concatenate([real, imag], axis=1).astype(BF16)


def regroup(parts):
    group = lax.broadcasted_iota(jnp.int32, parts[0].shape, 1) // 32
    for bit in range(2):
        step = 32 << bit
        upper = (group // (1 << bit)) % 2 == 1
        new = list(parts)
        for i in range(4):
            if i & (1 << bit):
                continue
            a, b = parts[i], parts[i | (1 << bit)]
            new[i] = jnp.where(upper, pltpu.roll(b, step, 1), a)
            new[i | (1 << bit)] = jnp.where(upper, b, pltpu.roll(a, LANES - step, 1))
        parts = new
    return parts


def regroup_plane(ref, t_ref, plane, rest_ref=None):
    def take(s, _):
        from_z = lax.div(s, YC) * (Z_LO * YC) + lax.rem(s, YC)
        if rest_ref is None:
            parts = [ref[from_z + z * YC] for z in range(Z_LO)]
        else:
            parts = [ref[from_z + z * YC] for z in range(Z_LO - 1)]
            shift = lax.rem(LANES - REST * lax.rem(s, YC), LANES)
            parts.append(pltpu.roll(rest_ref[lax.div(s, YC)], shift, 1))
        parts = [part.astype(F32) for part in regroup(parts)]
        for w in range(4):
            at = pl.ds(pl.multiple_of((s * 4 + w) * SLICE, SLICE), SLICE)
            t_ref[plane, 0, at] = parts[w][:SLICE]
            t_ref[plane, 1, at] = parts[w][SLICE:]
        return 0

    lax.fori_loop(0, 2 * YC, take, 0, unroll=16)


def columns(t_ref, plane, f):
    every = pl.ds(f, WINS_ALL, stride=SLICE)
    re, im = t_ref[plane, 0, every], t_ref[plane, 1, every]
    own = jnp.concatenate([re, im], axis=0)
    turned = jnp.concatenate([-im, re], axis=0)
    return own, jnp.concatenate([own, turned], axis=1).astype(BF16)


def gather_rest(near_ref, rest_ref):
    place = lax.broadcasted_iota(jnp.int32, (ROWS, LANES), 1) % 32 // REST
    for high in range(2):
        first = (high * Z_LO + Z_LO - 1) * YC
        rest = near_ref[first]
        for from_yc in range(1, YC):
            rest = jnp.where(place == from_yc, pltpu.roll(near_ref[first + from_yc], REST * from_yc, 1), rest)
        rest_ref[high] = rest


def near_pairs(t_ref, u_ref, left_ref):
    for f in range(SLICE):
        own, both = columns(t_ref, 0, f)
        left = own.T.astype(BF16)
        left_ref[f] = left
        pairs = dot(left, both, ((1,), (0,)))
        for part in range(2):
            u_ref[pl.ds(part * SLICE + f, LANES, stride=ROWS)] = pairs[:, part * LANES:(part + 1) * LANES]


def far_pairs(t_ref, u_ref, left_ref, both_ref, start, end, first):
    rows = lax.broadcasted_iota(jnp.int32, (end - start, LANES), 0) + start
    near = lax.broadcasted_iota(jnp.int32, (end - start, LANES), 1) > rows
    for f in range(SLICE):
        if first:
            both_ref[f] = columns(t_ref, 1, f)[1]
        pairs = dot(left_ref[f, start:end], both_ref[f], ((1,), (0,)))
        for part in range(2):
            at = pl.ds(start * ROWS + part * SLICE + f, end - start, stride=ROWS)
            u_ref[at] = jnp.where(near, u_ref[at], pairs[:, part * LANES:(part + 1) * LANES])


def round_rows(u_ref, s_ref, start, end):
    done = u_ref[start * ROWS:end * ROWS]
    s_ref[start // 2:end // 2] = done.astype(BF16).reshape((end - start) // 2, 2, ROWS, LANES)


def kernel(limit_hbm, live_hbm, x_hbm, tab_hbm, band_hbm, itab_hbm, out_ref,
           limit_ref, live_ref, x_ref, tab_ref, band_ref, itab_ref, w_ref, near_ref, far_ref, near_rest_ref, far_rest_ref, t_ref, u_ref, left_ref, both_ref, s_ref, got_ref,
           local_sem, send_sem, near_sem, far_sem, got_sem, rest_sem, ready_sem):
    chan, win = lax.axis_index("chan"), lax.axis_index("win")
    x = lax.div(chan, Z_LO)
    z, yc = lax.div(win, YC) * Z_LO + lax.rem(chan, Z_LO), lax.rem(win, YC)
    me = z * YC + yc
    has_left, has_right = x > 0, x < X - 1

    def device(to_x, to_z, to_yc):
        return {"chan": to_x * Z_LO + lax.rem(to_z, Z_LO), "win": lax.div(to_z, Z_LO) * YC + to_yc}

    loads = [
        pltpu.make_async_copy(src, dst, local_sem.at[i])
        for i, (src, dst) in enumerate(
            ((live_hbm, live_ref), (x_hbm, x_ref), (tab_hbm, tab_ref), (band_hbm, band_ref),
             (itab_hbm, itab_ref), (limit_hbm, limit_ref)))
    ]
    for load in loads[:4]:
        load.start()

    barrier = pltpu.get_barrier_semaphore()

    def signal(semaphore, to):
        pl.semaphore_signal(semaphore, inc=1, device_id=to, device_id_type=MESH)

    for step in range(1, Z):
        signal(barrier, device(x, lax.rem(z + step, Z), yc))
    for step in range(1, YC):
        signal(barrier, device(x, z, lax.rem(yc + step, YC)))

    @pl.when(has_right)
    def _():
        signal(barrier, device(x + 1, z, yc))

    for load in loads[4:]:
        load.start()
    lane = lax.rem(lax.broadcasted_iota(jnp.int32, (1, LANES), 1), 32)
    live = jnp.zeros((1, LANES), F32)
    loads[0].wait()
    for c in range(32):
        live = jnp.where(lane == c, live_ref[c].astype(F32), live)
    for load in loads[1:4]:
        load.wait()
    w_ref[...] = whiten(x_ref[...], live, tab_ref, band_ref[...])

    pl.semaphore_wait(barrier, Z - 1 + YC - 1 + has_left.astype(jnp.int32))
    for step in range(1, YC):
        signal(ready_sem, device(x, z, lax.rem(yc + step, YC)))

    own = pltpu.make_async_copy(w_ref.at[me], near_ref.at[me], local_sem.at[6])
    own.start()
    order = (0, 1, 7, 2, 6, 3, 5, 4)

    def send(to_z, to_yc):
        pltpu.make_async_remote_copy(
            src_ref=w_ref.at[to_z * YC + to_yc], dst_ref=near_ref.at[me], send_sem=send_sem,
            recv_sem=near_sem.at[z], device_id=device(x, to_z, to_yc), device_id_type=MESH,
        ).start()

    for step in order[1:]:
        send(lax.rem(z + step, Z), yc)
    for step in range(1, YC):
        send(z, lax.rem(yc + step, YC))
    pl.semaphore_wait(ready_sem, YC - 1)
    for step in order[1:]:
        to_z = lax.rem(z + step, Z)

        def send_on(i, _, to_z=to_z):
            send(to_z, lax.rem(yc + i, YC))
            return 0

        lax.fori_loop(1, YC, send_on, 0)

    @pl.when(jnp.logical_not(has_right))
    def _():
        far_ref[...] = jnp.zeros_like(far_ref)
        far_rest_ref[...] = jnp.zeros_like(far_rest_ref)

    own.wait()
    for step in order:
        from_z = lax.rem(z + Z - step, Z)
        chunk = pl.ds(from_z * YC, YC)
        some = near_ref.at[pl.ds(0, YC if step else YC - 1)]
        pltpu.make_async_copy(some, some, near_sem.at[from_z]).wait()

        @pl.when(jnp.logical_and(has_left, lax.rem(from_z, Z_LO) != Z_LO - 1))
        def _(chunk=chunk):
            pltpu.make_async_remote_copy(
                src_ref=near_ref.at[chunk], dst_ref=far_ref.at[chunk], send_sem=send_sem,
                recv_sem=far_sem, device_id=device(x - 1, z, yc), device_id_type=MESH,
            ).start()

    @pl.when(has_left)
    def _():
        gather_rest(near_ref, near_rest_ref)
        pltpu.make_async_remote_copy(
            src_ref=near_rest_ref, dst_ref=far_rest_ref, send_sem=send_sem,
            recv_sem=rest_sem, device_id=device(x - 1, z, yc), device_id_type=MESH,
        ).start()

    def give(start, end):
        round_rows(u_ref, s_ref, start, end)
        first, count = start // 2, (end - start) // 2

        def go(i, _):
            pair = first + lax.rem(i + z * 2 + yc, count)
            to_z = lax.div(lax.rem(pair, 2 * YC), YC) * Z_LO + lax.div(pair, 2 * YC)
            to_yc = lax.rem(pair, YC)

            @pl.when(to_z * YC + to_yc != me)
            def _():
                pltpu.make_async_remote_copy(
                    src_ref=s_ref.at[pair], dst_ref=got_ref.at[me], send_sem=send_sem,
                    recv_sem=got_sem, device_id=device(x, to_z, to_yc), device_id_type=MESH,
                ).start()
            return 0

        lax.fori_loop(0, count, go, 0)

    regroup_plane(near_ref, t_ref, 0)
    near_pairs(t_ref, u_ref, left_ref)
    give(0, EARLY)

    @pl.when(has_right)
    def _():
        whole = far_ref.at[pl.ds(0, 2 * (Z_LO - 1) * YC)]
        pltpu.make_async_copy(whole, whole, far_sem).wait()
        pltpu.make_async_copy(far_rest_ref, far_rest_ref, rest_sem).wait()

    regroup_plane(far_ref, t_ref, 1, far_rest_ref)
    for start, send_start, end in BLOCKS:
        far_pairs(t_ref, u_ref, left_ref, both_ref, start, end, start == BLOCKS[0][0])
        give(send_start, end)

    owned = lax.rem(z, Z_LO) * (2 * YC) + lax.div(z, Z_LO) * YC + yc
    own = pltpu.make_async_copy(s_ref.at[owned], got_ref.at[me], local_sem.at[7])
    own.start()
    own.wait()
    loads[4].wait()
    loads[5].wait()
    rest = got_ref.at[pl.ds(0, PLANE - 1)]
    pltpu.make_async_copy(rest, rest, got_sem).wait()

    right = jnp.concatenate([got_ref[:, c].reshape(SAMPLES, LANES) for c in range(2)], axis=1)
    pairs = dot(itab_ref[0], right, ((1,), (0,)))
    for term in range(1, itab_ref.shape[0]):
        pairs = pairs + dot(itab_ref[term], right, ((1,), (0,)))
    offsets = lax.broadcasted_iota(jnp.int32, (LAGS_PAD, LANES), 1) + 1
    first = lax.rem(chan, Z_LO) * 32 + win * 2
    for c in range(2):
        reach = jnp.minimum(limit_ref[win * 2 + c], CHANNELS - 1 - (chan * 32 + win * 2 + c))
        kept = pltpu.roll(pairs[:, c * LANES:(c + 1) * LANES], LANES - 1 - c - first, 1)
        out_ref[pl.ds(c, LAGS_PAD, stride=2)] = jnp.where(offsets <= reach, kept, 0.0)

    sent = w_ref.at[pl.ds(0, PLANE - 1)]
    pltpu.make_async_copy(sent, sent, send_sem).wait()
    pltpu.make_async_copy(rest, rest, send_sem).wait()

    @pl.when(has_left)
    def _():
        whole = far_ref.at[pl.ds(0, 2 * (Z_LO - 1) * YC)]
        pltpu.make_async_copy(whole, whole, send_sem).wait()
        pltpu.make_async_copy(near_rest_ref, near_rest_ref, send_sem).wait()


def shards(records, live, band_limit):
    tab = jnp.asarray(forward_tables(2))
    band = jnp.asarray(band_table())
    itab = jnp.asarray(inverse_tables(2))
    rows = records.reshape(LANES, SAMPLES)
    vmem, hbm = pl.BlockSpec(memory_space=pltpu.VMEM), pl.BlockSpec(memory_space=pltpu.HBM)
    out = pl.pallas_call(
        kernel,
        out_shape=jax.ShapeDtypeStruct((2 * LAGS_PAD, LANES), F32),
        in_specs=[hbm] * 6,
        out_specs=vmem,
        scratch_shapes=[
            pltpu.SMEM(band_limit.shape, jnp.int32),
            pltpu.SMEM(live.shape, jnp.int32),
            pltpu.VMEM(rows.shape, BF16),
            pltpu.VMEM(tab.shape, BF16),
            pltpu.VMEM(band.shape, BF16),
            pltpu.VMEM(itab.shape, BF16),
            pltpu.VMEM((PLANE, ROWS, LANES), BF16),
            pltpu.VMEM((PLANE, ROWS, LANES), BF16),
            pltpu.VMEM((PLANE, ROWS, LANES), BF16),
            pltpu.VMEM((2, ROWS, LANES), BF16),
            pltpu.VMEM((2, ROWS, LANES), BF16),
            pltpu.VMEM((2, 2, WINS_ALL * SLICE, LANES), F32),
            pltpu.VMEM((LANES * ROWS, LANES), F32),
            pltpu.VMEM((SLICE, LANES, LANES), BF16),
            pltpu.VMEM((SLICE, LANES, 2 * LANES), BF16),
            pltpu.VMEM((PLANE, 2, ROWS, LANES), BF16),
            pltpu.VMEM((PLANE, 2, ROWS, LANES), BF16),
            pltpu.SemaphoreType.DMA((8,)),
            pltpu.SemaphoreType.DMA,
            pltpu.SemaphoreType.DMA((Z,)),
            pltpu.SemaphoreType.DMA,
            pltpu.SemaphoreType.DMA,
            pltpu.SemaphoreType.DMA,
            pltpu.SemaphoreType.REGULAR,
        ],
        compiler_params=pltpu.CompilerParams(
            collective_id=0, has_side_effects=True, vmem_limit_bytes=40 << 20
        ),
        cost_estimate=pl.CostEstimate(flops=1_500_000_000, bytes_accessed=8_000_000, transcendentals=65536),
        name="correlate",
    )(*[pltpu.with_memory_space_constraint(a, pltpu.HBM) for a in (band_limit, live, rows, tab, band, itab)])
    out = out.reshape(LAGS_PAD, 2, LANES)[:LAGS, :, :R]
    return jnp.transpose(out, (1, 2, 0))


def solution(mesh):
    placed = (P("win", "chan", None), P("chan"), P("chan"))
    return jax.shard_map(
        shards,
        mesh=mesh,
        in_specs=placed,
        out_specs=P(("chan", "win"), None, None),
        check_vma=False,
    )
```

```python
import math

import jax
import jax.numpy as jnp
import ml_dtypes
import numpy as np
from jax import lax
from jax.experimental import pallas as pl
from jax.experimental.pallas import tpu as pltpu
from jax.sharding import PartitionSpec as P

R = 100
LANES = 128
HALF_LAG = 128
HALF_WIN = 32
SAMPLES = 1024
BINS = SAMPLES // 2
LAGS = 2 * HALF_LAG + 1
WINS_ALL = 64
CHANNELS = 512

LAGS_PAD = 272
X, Z_LO, Z, YC = 4, 4, 8, 8
PLANE = Z * YC
SLICE = BINS // PLANE
EARLY = (LANES - R) // 4 * 4
BLOCKS = ((16, EARLY, 64), (64, 64, 96), (96, 96, 128))
ROWS = 2 * SLICE
REST = R - (Z_LO - 1) * 32

MESH = pl.DeviceIdType.MESH
F32, BF16 = jnp.float32, jnp.bfloat16


def split(table, terms):
    parts, rest = [], table.astype(np.float64)
    for _ in range(terms):
        part = rest.astype(np.float32).astype(ml_dtypes.bfloat16)
        parts.append(part)
        rest = rest - part.astype(np.float64)
    return parts


RESIDUES = (0, 4, 1, 7, 2, 6, 3, 5)
RUN = BINS // 8
ORDER = np.concatenate([np.arange(RUN) * 8 + (r or 8) for r in RESIDUES])


def forward_tables(terms):
    groups = []
    for g in range(4):
        halves = []
        for side in range(2):
            freqs = ORDER[(2 * g + side) * RUN:(2 * g + side + 1) * RUN, None]
            phase = np.mod(freqs * np.arange(LANES)[None, :], SAMPLES) * (2.0 * math.pi / SAMPLES)
            cos, sin = np.cos(phase), np.sin(phase)
            if g == 0:
                real, imag = [np.zeros_like(cos)] * 2, [np.zeros_like(cos)] * 2
                real[side], imag[side] = cos, -sin
            else:
                sign = 1 - 2 * side
                real, imag = [cos, sign * sin], [-sin, sign * cos]
            halves.append((np.concatenate(real, axis=1), np.concatenate(imag, axis=1)))
        (real_a, imag_a), (real_b, imag_b) = halves
        groups.append(np.concatenate([real_a, real_b, imag_a, imag_b], axis=0))
    return np.stack(split(np.stack(groups), terms))


def inverse_tables(terms):
    freqs = ORDER[:, None]
    shifts = np.arange(LAGS)[None, :] - HALF_LAG
    phase = np.mod(freqs * shifts, SAMPLES) * (2.0 * math.pi / SAMPLES)
    factor = 2.0 / math.sqrt(SAMPLES * WINS_ALL)
    real = (np.cos(phase) * factor).reshape(PLANE, SLICE, LAGS)
    imag = (-np.sin(phase) * factor).reshape(PLANE, SLICE, LAGS)
    table = np.concatenate([real, imag], axis=1).reshape(SAMPLES, LAGS).T
    table = np.pad(table, ((0, LAGS_PAD - LAGS), (0, 0)))
    return np.stack(split(table, terms))


def band_table():
    return (np.abs(ORDER[:, None] - ORDER[None, :]) <= HALF_WIN).astype(ml_dtypes.bfloat16)


def dot(a, b, dims):
    return lax.dot_general(a, b, (dims, ((), ())), preferred_element_type=F32)


def residue_sums(x):
    b = [x[:, LANES * i:LANES * (i + 1)].astype(F32) for i in range(8)]
    plus = [b[i] + b[i + 4] for i in range(4)]
    minus = [b[i] - b[i + 4] for i in range(4)]
    even, odd = plus[0] + plus[2], plus[1] + plus[3]
    root = math.sqrt(0.5)
    across, along = (minus[1] - minus[3]) * root, (minus[1] + minus[3]) * root
    return (
        (even + odd, even - odd),
        (minus[0] + across, -minus[2] - along),
        (plus[0] - plus[2], plus[3] - plus[1]),
        (minus[0] - across, minus[2] - along),
    )


def whiten(x, live, tab_ref, band):
    real, imag = [], []
    for g, sums in enumerate(residue_sums(x)):
        sums = jnp.concatenate(sums, axis=1)
        high = sums.astype(BF16)
        low = (sums - high.astype(F32)).astype(BF16)
        spec = dot(tab_ref[0, g], high, ((1,), (1,)))
        spec = spec + dot(tab_ref[0, g], low, ((1,), (1,)))
        spec = spec + dot(tab_ref[1, g], high, ((1,), (1,)))
        real.append(spec[:2 * RUN])
        imag.append(spec[2 * RUN:])
    real, imag = jnp.concatenate(real, axis=0), jnp.concatenate(imag, axis=0)
    amplitude = jnp.sqrt(real * real + imag * imag)
    high = amplitude.astype(BF16)
    low = (amplitude - high.astype(F32)).astype(BF16)
    near = dot(band, high, ((1,), (0,))) + dot(band, low, ((1,), (0,)))
    factor = live / (near * (1.0 / (2 * HALF_WIN + 1)) + 1e-06)
    real = (real * factor).reshape(PLANE, SLICE, LANES)
    imag = (imag * factor).reshape(PLANE, SLICE, LANES)
    return jnp.concatenate([real, imag], axis=1).astype(BF16)


def regroup(parts):
    group = lax.broadcasted_iota(jnp.int32, parts[0].shape, 1) // 32
    for bit in range(2):
        step = 32 << bit
        upper = (group // (1 << bit)) % 2 == 1
        new = list(parts)
        for i in range(4):
            if i & (1 << bit):
                continue
            a, b = parts[i], parts[i | (1 << bit)]
            new[i] = jnp.where(upper, pltpu.roll(b, step, 1), a)
            new[i | (1 << bit)] = jnp.where(upper, b, pltpu.roll(a, LANES - step, 1))
        parts = new
    return parts


def regroup_plane(ref, t_ref, plane, rest_ref=None):
    def take(s, _):
        from_z = lax.div(s, YC) * (Z_LO * YC) + lax.rem(s, YC)
        if rest_ref is None:
            parts = [ref[from_z + z * YC] for z in range(Z_LO)]
        else:
            parts = [ref[from_z + z * YC] for z in range(Z_LO - 1)]
            shift = lax.rem(LANES - REST * lax.rem(s, YC), LANES)
            parts.append(pltpu.roll(rest_ref[lax.div(s, YC)], shift, 1))
        parts = [part.astype(F32) for part in regroup(parts)]
        for w in range(4):
            at = pl.ds(pl.multiple_of((s * 4 + w) * SLICE, SLICE), SLICE)
            t_ref[plane, 0, at] = parts[w][:SLICE]
            t_ref[plane, 1, at] = parts[w][SLICE:]
        return 0

    lax.fori_loop(0, 2 * YC, take, 0, unroll=16)


def columns(t_ref, plane, f):
    every = pl.ds(f, WINS_ALL, stride=SLICE)
    re, im = t_ref[plane, 0, every], t_ref[plane, 1, every]
    own = jnp.concatenate([re, im], axis=0)
    turned = jnp.concatenate([-im, re], axis=0)
    return own, jnp.concatenate([own, turned], axis=1).astype(BF16)


def gather_rest(near_ref, rest_ref):
    place = lax.broadcasted_iota(jnp.int32, (ROWS, LANES), 1) % 32 // REST
    for high in range(2):
        first = (high * Z_LO + Z_LO - 1) * YC
        rest = near_ref[first]
        for from_yc in range(1, YC):
            rest = jnp.where(place == from_yc, pltpu.roll(near_ref[first + from_yc], REST * from_yc, 1), rest)
        rest_ref[high] = rest


def near_pairs(t_ref, u_ref, left_ref):
    for f in range(SLICE):
        own, both = columns(t_ref, 0, f)
        left = own.T.astype(BF16)
        left_ref[f] = left
        pairs = dot(left, both, ((1,), (0,)))
        for part in range(2):
            u_ref[pl.ds(part * SLICE + f, LANES, stride=ROWS)] = pairs[:, part * LANES:(part + 1) * LANES]


def far_pairs(t_ref, u_ref, left_ref, both_ref, start, end, first):
    rows = lax.broadcasted_iota(jnp.int32, (end - start, LANES), 0) + start
    near = lax.broadcasted_iota(jnp.int32, (end - start, LANES), 1) > rows
    for f in range(SLICE):
        if first:
            both_ref[f] = columns(t_ref, 1, f)[1]
        pairs = dot(left_ref[f, start:end], both_ref[f], ((1,), (0,)))
        for part in range(2):
            at = pl.ds(start * ROWS + part * SLICE + f, end - start, stride=ROWS)
            u_ref[at] = jnp.where(near, u_ref[at], pairs[:, part * LANES:(part + 1) * LANES])


def round_rows(u_ref, s_ref, start, end):
    done = u_ref[start * ROWS:end * ROWS]
    s_ref[start // 2:end // 2] = done.astype(BF16).reshape((end - start) // 2, 2, ROWS, LANES)


def kernel(limit_hbm, live_hbm, x_hbm, tab_hbm, band_hbm, itab_hbm, out_ref,
           limit_ref, live_ref, x_ref, tab_ref, band_ref, itab_ref, w_ref, near_ref, far_ref, near_rest_ref, far_rest_ref, t_ref, u_ref, left_ref, both_ref, s_ref, got_ref,
           local_sem, send_sem, near_sem, far_sem, got_sem, rest_sem, ready_sem):
    chan, win = lax.axis_index("chan"), lax.axis_index("win")
    x = lax.div(chan, Z_LO)
    z, yc = lax.div(win, YC) * Z_LO + lax.rem(chan, Z_LO), lax.rem(win, YC)
    me = z * YC + yc
    has_left, has_right = x > 0, x < X - 1

    def device(to_x, to_z, to_yc):
        return {"chan": to_x * Z_LO + lax.rem(to_z, Z_LO), "win": lax.div(to_z, Z_LO) * YC + to_yc}

    loads = [
        pltpu.make_async_copy(src, dst, local_sem.at[i])
        for i, (src, dst) in enumerate(
            ((live_hbm, live_ref), (x_hbm, x_ref), (tab_hbm, tab_ref), (band_hbm, band_ref),
             (itab_hbm, itab_ref), (limit_hbm, limit_ref)))
    ]
    for load in loads[:4]:
        load.start()

    barrier = pltpu.get_barrier_semaphore()

    def signal(semaphore, to):
        pl.semaphore_signal(semaphore, inc=1, device_id=to, device_id_type=MESH)

    for step in range(1, Z):
        signal(barrier, device(x, lax.rem(z + step, Z), yc))
    for step in range(1, YC):
        signal(barrier, device(x, z, lax.rem(yc + step, YC)))

    @pl.when(has_right)
    def _():
        signal(barrier, device(x + 1, z, yc))

    for load in loads[4:]:
        load.start()
    lane = lax.rem(lax.broadcasted_iota(jnp.int32, (1, LANES), 1), 32)
    live = jnp.zeros((1, LANES), F32)
    loads[0].wait()
    for c in range(32):
        live = jnp.where(lane == c, live_ref[c].astype(F32), live)
    for load in loads[1:4]:
        load.wait()
    w_ref[...] = whiten(x_ref[...], live, tab_ref, band_ref[...])

    pl.semaphore_wait(barrier, Z - 1 + YC - 1 + has_left.astype(jnp.int32))
    for step in range(1, YC):
        signal(ready_sem, device(x, z, lax.rem(yc + step, YC)))

    own = pltpu.make_async_copy(w_ref.at[me], near_ref.at[me], local_sem.at[6])
    own.start()
    order = (0, 1, 7, 2, 6, 3, 5, 4)

    def send(to_z, to_yc):
        pltpu.make_async_remote_copy(
            src_ref=w_ref.at[to_z * YC + to_yc], dst_ref=near_ref.at[me], send_sem=send_sem,
            recv_sem=near_sem.at[z], device_id=device(x, to_z, to_yc), device_id_type=MESH,
        ).start()

    for step in order[1:]:
        send(lax.rem(z + step, Z), yc)
    for step in range(1, YC):
        send(z, lax.rem(yc + step, YC))
    pl.semaphore_wait(ready_sem, YC - 1)
    for step in order[1:]:
        to_z = lax.rem(z + step, Z)

        def send_on(i, _, to_z=to_z):
            send(to_z, lax.rem(yc + i, YC))
            return 0

        lax.fori_loop(1, YC, send_on, 0)

    @pl.when(jnp.logical_not(has_right))
    def _():
        far_ref[...] = jnp.zeros_like(far_ref)
        far_rest_ref[...] = jnp.zeros_like(far_rest_ref)

    own.wait()
    for step in order:
        from_z = lax.rem(z + Z - step, Z)
        chunk = pl.ds(from_z * YC, YC)
        some = near_ref.at[pl.ds(0, YC if step else YC - 1)]
        pltpu.make_async_copy(some, some, near_sem.at[from_z]).wait()

        @pl.when(jnp.logical_and(has_left, lax.rem(from_z, Z_LO) != Z_LO - 1))
        def _(chunk=chunk):
            pltpu.make_async_remote_copy(
                src_ref=near_ref.at[chunk], dst_ref=far_ref.at[chunk], send_sem=send_sem,
                recv_sem=far_sem, device_id=device(x - 1, z, yc), device_id_type=MESH,
            ).start()

    @pl.when(has_left)
    def _():
        gather_rest(near_ref, near_rest_ref)
        pltpu.make_async_remote_copy(
            src_ref=near_rest_ref, dst_ref=far_rest_ref, send_sem=send_sem,
            recv_sem=rest_sem, device_id=device(x - 1, z, yc), device_id_type=MESH,
        ).start()

    def give(start, end):
        round_rows(u_ref, s_ref, start, end)
        first, count = start // 2, (end - start) // 2

        def go(i, _):
            pair = first + lax.rem(i + z * 2 + yc, count)
            to_z = lax.div(lax.rem(pair, 2 * YC), YC) * Z_LO + lax.div(pair, 2 * YC)
            to_yc = lax.rem(pair, YC)

            @pl.when(to_z * YC + to_yc != me)
            def _():
                pltpu.make_async_remote_copy(
                    src_ref=s_ref.at[pair], dst_ref=got_ref.at[me], send_sem=send_sem,
                    recv_sem=got_sem, device_id=device(x, to_z, to_yc), device_id_type=MESH,
                ).start()
            return 0

        lax.fori_loop(0, count, go, 0)

    regroup_plane(near_ref, t_ref, 0)
    near_pairs(t_ref, u_ref, left_ref)
    give(0, EARLY)

    @pl.when(has_right)
    def _():
        whole = far_ref.at[pl.ds(0, 2 * (Z_LO - 1) * YC)]
        pltpu.make_async_copy(whole, whole, far_sem).wait()
        pltpu.make_async_copy(far_rest_ref, far_rest_ref, rest_sem).wait()

    regroup_plane(far_ref, t_ref, 1, far_rest_ref)
    for start, send_start, end in BLOCKS:
        far_pairs(t_ref, u_ref, left_ref, both_ref, start, end, start == BLOCKS[0][0])
        give(send_start, end)

    owned = lax.rem(z, Z_LO) * (2 * YC) + lax.div(z, Z_LO) * YC + yc
    own = pltpu.make_async_copy(s_ref.at[owned], got_ref.at[me], local_sem.at[7])
    own.start()
    own.wait()
    loads[4].wait()
    loads[5].wait()
    rest = got_ref.at[pl.ds(0, PLANE - 1)]
    pltpu.make_async_copy(rest, rest, got_sem).wait()

    right = jnp.concatenate([got_ref[:, c].reshape(SAMPLES, LANES) for c in range(2)], axis=1)
    pairs = dot(itab_ref[0], right, ((1,), (0,)))
    for term in range(1, itab_ref.shape[0]):
        pairs = pairs + dot(itab_ref[term], right, ((1,), (0,)))
    offsets = lax.broadcasted_iota(jnp.int32, (LAGS_PAD, LANES), 1) + 1
    first = lax.rem(chan, Z_LO) * 32 + win * 2
    for c in range(2):
        reach = jnp.minimum(limit_ref[win * 2 + c], CHANNELS - 1 - (chan * 32 + win * 2 + c))
        kept = pltpu.roll(pairs[:, c * LANES:(c + 1) * LANES], LANES - 1 - c - first, 1)
        out_ref[pl.ds(c, LAGS_PAD - 8, stride=2)] = jnp.where(offsets <= reach, kept, 0.0)[:LAGS_PAD - 8]

    sent = w_ref.at[pl.ds(0, PLANE - 1)]
    pltpu.make_async_copy(sent, sent, send_sem).wait()
    pltpu.make_async_copy(rest, rest, send_sem).wait()

    @pl.when(has_left)
    def _():
        whole = far_ref.at[pl.ds(0, 2 * (Z_LO - 1) * YC)]
        pltpu.make_async_copy(whole, whole, send_sem).wait()
        pltpu.make_async_copy(near_rest_ref, near_rest_ref, send_sem).wait()


def shards(records, live, band_limit):
    tab = jnp.asarray(forward_tables(2))
    band = jnp.asarray(band_table())
    itab = jnp.asarray(inverse_tables(2))
    rows = records.reshape(LANES, SAMPLES)
    vmem, hbm = pl.BlockSpec(memory_space=pltpu.VMEM), pl.BlockSpec(memory_space=pltpu.HBM)
    out = pl.pallas_call(
        kernel,
        out_shape=jax.ShapeDtypeStruct((2 * LAGS_PAD, LANES), F32),
        in_specs=[hbm] * 6,
        out_specs=vmem,
        scratch_shapes=[
            pltpu.SMEM(band_limit.shape, jnp.int32),
            pltpu.SMEM(live.shape, jnp.int32),
            pltpu.VMEM(rows.shape, BF16),
            pltpu.VMEM(tab.shape, BF16),
            pltpu.VMEM(band.shape, BF16),
            pltpu.VMEM(itab.shape, BF16),
            pltpu.VMEM((PLANE, ROWS, LANES), BF16),
            pltpu.VMEM((PLANE, ROWS, LANES), BF16),
            pltpu.VMEM((PLANE, ROWS, LANES), BF16),
            pltpu.VMEM((2, ROWS, LANES), BF16),
            pltpu.VMEM((2, ROWS, LANES), BF16),
            pltpu.VMEM((2, 2, (WINS_ALL + 1) * SLICE, LANES), F32),
            pltpu.VMEM(((LANES + 1) * ROWS, LANES), F32),
            pltpu.VMEM((SLICE, LANES, LANES), BF16),
            pltpu.VMEM((SLICE, LANES, 2 * LANES), BF16),
            pltpu.VMEM((PLANE, 2, ROWS, LANES), BF16),
            pltpu.VMEM((PLANE, 2, ROWS, LANES), BF16),
            pltpu.SemaphoreType.DMA((8,)),
            pltpu.SemaphoreType.DMA,
            pltpu.SemaphoreType.DMA((Z,)),
            pltpu.SemaphoreType.DMA,
            pltpu.SemaphoreType.DMA,
            pltpu.SemaphoreType.DMA,
            pltpu.SemaphoreType.REGULAR,
        ],
        compiler_params=pltpu.CompilerParams(
            collective_id=0, has_side_effects=True, vmem_limit_bytes=40 << 20
        ),
        cost_estimate=pl.CostEstimate(flops=1_500_000_000, bytes_accessed=8_000_000, transcendentals=65536),
        name="correlate",
    )(*[pltpu.with_memory_space_constraint(a, pltpu.HBM) for a in (band_limit, live, rows, tab, band, itab)])
    out = out.reshape(LAGS_PAD, 2, LANES)[:LAGS, :, :R]
    return jnp.transpose(out, (1, 2, 0))


def solution(mesh):
    placed = (P("win", "chan", None), P("chan"), P("chan"))
    return jax.shard_map(
        shards,
        mesh=mesh,
        in_specs=placed,
        out_specs=P(("chan", "win"), None, None),
        check_vma=False,
    )
```

```python
import math

import jax
import jax.numpy as jnp
import ml_dtypes
import numpy as np
from jax import lax
from jax.experimental import pallas as pl
from jax.experimental.pallas import tpu as pltpu
from jax.sharding import PartitionSpec as P

R = 100
LANES = 128
HALF_LAG = 128
HALF_WIN = 32
SAMPLES = 1024
BINS = SAMPLES // 2
LAGS = 2 * HALF_LAG + 1
WINS_ALL = 64
CHANNELS = 512

LAGS_PAD = 272
X, Z_LO, Z, YC = 4, 4, 8, 8
PLANE = Z * YC
SLICE = BINS // PLANE
EARLY = (LANES - R) // 4 * 4
BLOCKS = ((16, EARLY, 64), (64, 64, 96), (96, 96, 128))
ROWS = 2 * SLICE
REST = R - (Z_LO - 1) * 32

MESH = pl.DeviceIdType.MESH
F32, BF16 = jnp.float32, jnp.bfloat16


def split(table, terms):
    parts, rest = [], table.astype(np.float64)
    for _ in range(terms):
        part = rest.astype(np.float32).astype(ml_dtypes.bfloat16)
        parts.append(part)
        rest = rest - part.astype(np.float64)
    return parts


RESIDUES = (0, 4, 1, 7, 2, 6, 3, 5)
RUN = BINS // 8
ORDER = np.concatenate([np.arange(RUN) * 8 + (r or 8) for r in RESIDUES])


def forward_tables(terms):
    groups = []
    for g in range(4):
        halves = []
        for side in range(2):
            freqs = ORDER[(2 * g + side) * RUN:(2 * g + side + 1) * RUN, None]
            phase = np.mod(freqs * np.arange(LANES)[None, :], SAMPLES) * (2.0 * math.pi / SAMPLES)
            cos, sin = np.cos(phase), np.sin(phase)
            if g == 0:
                real, imag = [np.zeros_like(cos)] * 2, [np.zeros_like(cos)] * 2
                real[side], imag[side] = cos, -sin
            else:
                sign = 1 - 2 * side
                real, imag = [cos, sign * sin], [-sin, sign * cos]
            halves.append((np.concatenate(real, axis=1), np.concatenate(imag, axis=1)))
        (real_a, imag_a), (real_b, imag_b) = halves
        groups.append(np.concatenate([real_a, real_b, imag_a, imag_b], axis=0))
    return np.stack(split(np.stack(groups), terms))


def inverse_tables(terms):
    freqs = ORDER[:, None]
    shifts = np.arange(LAGS)[None, :] - HALF_LAG
    phase = np.mod(freqs * shifts, SAMPLES) * (2.0 * math.pi / SAMPLES)
    factor = 2.0 / math.sqrt(SAMPLES * WINS_ALL)
    real = (np.cos(phase) * factor).reshape(PLANE, SLICE, LAGS)
    imag = (-np.sin(phase) * factor).reshape(PLANE, SLICE, LAGS)
    table = np.concatenate([real, imag], axis=1).reshape(SAMPLES, LAGS).T
    table = np.pad(table, ((0, LAGS_PAD - LAGS), (0, 0)))
    return np.stack(split(table, terms))


def band_table():
    return (np.abs(ORDER[:, None] - ORDER[None, :]) <= HALF_WIN).astype(ml_dtypes.bfloat16)


def dot(a, b, dims):
    return lax.dot_general(a, b, (dims, ((), ())), preferred_element_type=F32)


def residue_sums(x):
    b = [x[:, LANES * i:LANES * (i + 1)].astype(F32) for i in range(8)]
    plus = [b[i] + b[i + 4] for i in range(4)]
    minus = [b[i] - b[i + 4] for i in range(4)]
    even, odd = plus[0] + plus[2], plus[1] + plus[3]
    root = math.sqrt(0.5)
    across, along = (minus[1] - minus[3]) * root, (minus[1] + minus[3]) * root
    return (
        (even + odd, even - odd),
        (minus[0] + across, -minus[2] - along),
        (plus[0] - plus[2], plus[3] - plus[1]),
        (minus[0] - across, minus[2] - along),
    )


def whiten(x, live, tab_ref, band):
    real, imag = [], []
    for g, sums in enumerate(residue_sums(x)):
        sums = jnp.concatenate(sums, axis=1)
        high = sums.astype(BF16)
        low = (sums - high.astype(F32)).astype(BF16)
        spec = dot(tab_ref[0, g], high, ((1,), (1,)))
        spec = spec + dot(tab_ref[0, g], low, ((1,), (1,)))
        spec = spec + dot(tab_ref[1, g], high, ((1,), (1,)))
        real.append(spec[:2 * RUN])
        imag.append(spec[2 * RUN:])
    real, imag = jnp.concatenate(real, axis=0), jnp.concatenate(imag, axis=0)
    amplitude = jnp.sqrt(real * real + imag * imag)
    high = amplitude.astype(BF16)
    low = (amplitude - high.astype(F32)).astype(BF16)
    near = dot(band, high, ((1,), (0,))) + dot(band, low, ((1,), (0,)))
    factor = live / (near * (1.0 / (2 * HALF_WIN + 1)) + 1e-06)
    real = (real * factor).reshape(PLANE, SLICE, LANES)
    imag = (imag * factor).reshape(PLANE, SLICE, LANES)
    return jnp.concatenate([real, imag], axis=1).astype(BF16)


def regroup(parts):
    group = lax.broadcasted_iota(jnp.int32, parts[0].shape, 1) // 32
    for bit in range(2):
        step = 32 << bit
        upper = (group // (1 << bit)) % 2 == 1
        new = list(parts)
        for i in range(4):
            if i & (1 << bit):
                continue
            a, b = parts[i], parts[i | (1 << bit)]
            new[i] = jnp.where(upper, pltpu.roll(b, step, 1), a)
            new[i | (1 << bit)] = jnp.where(upper, b, pltpu.roll(a, LANES - step, 1))
        parts = new
    return parts


def regroup_plane(ref, t_ref, plane, rest_ref=None):
    def take(s, _):
        from_z = lax.div(s, YC) * (Z_LO * YC) + lax.rem(s, YC)
        if rest_ref is None:
            parts = [ref[from_z + z * YC] for z in range(Z_LO)]
        else:
            parts = [ref[from_z + z * YC] for z in range(Z_LO - 1)]
            shift = lax.rem(LANES - REST * lax.rem(s, YC), LANES)
            parts.append(pltpu.roll(rest_ref[lax.div(s, YC)], shift, 1))
        parts = [part.astype(F32) for part in regroup(parts)]
        for w in range(4):
            at = pl.ds(pl.multiple_of((s * 4 + w) * SLICE, SLICE), SLICE)
            t_ref[plane, 0, at] = parts[w][:SLICE]
            t_ref[plane, 1, at] = parts[w][SLICE:]
        return 0

    lax.fori_loop(0, 2 * YC, take, 0, unroll=16)


def columns(t_ref, plane, f):
    every = pl.ds(f, WINS_ALL, stride=SLICE)
    re, im = t_ref[plane, 0, every], t_ref[plane, 1, every]
    own = jnp.concatenate([re, im], axis=0)
    turned = jnp.concatenate([-im, re], axis=0)
    return own, jnp.concatenate([own, turned], axis=1).astype(BF16)


def gather_rest(near_ref, rest_ref):
    place = lax.broadcasted_iota(jnp.int32, (ROWS, LANES), 1) % 32 // REST
    for high in range(2):
        first = (high * Z_LO + Z_LO - 1) * YC
        rest = near_ref[first]
        for from_yc in range(1, YC):
            rest = jnp.where(place == from_yc, pltpu.roll(near_ref[first + from_yc], REST * from_yc, 1), rest)
        rest_ref[high] = rest


def near_pairs(t_ref, u_ref, left_ref):
    for f in range(SLICE):
        own, both = columns(t_ref, 0, f)
        left = own.T.astype(BF16)
        left_ref[f] = left
        pairs = dot(left, both, ((1,), (0,)))
        for part in range(2):
            u_ref[pl.ds(part * SLICE + f, LANES, stride=ROWS)] = pairs[:, part * LANES:(part + 1) * LANES]


def far_pairs(t_ref, u_ref, left_ref, both_ref, start, end, first):
    rows = lax.broadcasted_iota(jnp.int32, (end - start, LANES), 0) + start
    near = lax.broadcasted_iota(jnp.int32, (end - start, LANES), 1) > rows
    for f in range(SLICE):
        if first:
            both_ref[f] = columns(t_ref, 1, f)[1]
        pairs = dot(left_ref[f, start:end], both_ref[f], ((1,), (0,)))
        for part in range(2):
            at = pl.ds(start * ROWS + part * SLICE + f, end - start, stride=ROWS)
            u_ref[at] = jnp.where(near, u_ref[at], pairs[:, part * LANES:(part + 1) * LANES])


def round_rows(u_ref, s_ref, start, end):
    done = u_ref[start * ROWS:end * ROWS]
    s_ref[start // 2:end // 2] = done.astype(BF16).reshape((end - start) // 2, 2, ROWS, LANES)


def kernel(limit_hbm, live_hbm, x_hbm, tab_hbm, band_hbm, itab_hbm, out_ref,
           limit_ref, live_ref, x_ref, tab_ref, band_ref, itab_ref, w_ref, near_ref, far_ref, near_rest_ref, far_rest_ref, t_ref, u_ref, left_ref, both_ref, s_ref, got_ref,
           local_sem, send_sem, near_sem, far_sem, got_sem, rest_sem, ready_sem):
    chan, win = lax.axis_index("chan"), lax.axis_index("win")
    x = lax.div(chan, Z_LO)
    z, yc = lax.div(win, YC) * Z_LO + lax.rem(chan, Z_LO), lax.rem(win, YC)
    me = z * YC + yc
    has_left, has_right = x > 0, x < X - 1

    def device(to_x, to_z, to_yc):
        return {"chan": to_x * Z_LO + lax.rem(to_z, Z_LO), "win": lax.div(to_z, Z_LO) * YC + to_yc}

    loads = [
        pltpu.make_async_copy(src, dst, local_sem.at[i])
        for i, (src, dst) in enumerate(
            ((live_hbm, live_ref), (x_hbm, x_ref), (tab_hbm, tab_ref), (band_hbm, band_ref),
             (itab_hbm, itab_ref), (limit_hbm, limit_ref)))
    ]
    for load in loads[:4]:
        load.start()

    barrier = pltpu.get_barrier_semaphore()

    def signal(semaphore, to):
        pl.semaphore_signal(semaphore, inc=1, device_id=to, device_id_type=MESH)

    for step in range(1, Z):
        signal(barrier, device(x, lax.rem(z + step, Z), yc))
    for step in range(1, YC):
        signal(barrier, device(x, z, lax.rem(yc + step, YC)))

    @pl.when(has_right)
    def _():
        signal(barrier, device(x + 1, z, yc))

    for load in loads[4:]:
        load.start()
    lane = lax.rem(lax.broadcasted_iota(jnp.int32, (1, LANES), 1), 32)
    live = jnp.zeros((1, LANES), F32)
    loads[0].wait()
    for c in range(32):
        live = jnp.where(lane == c, live_ref[c].astype(F32), live)
    for load in loads[1:4]:
        load.wait()
    w_ref[...] = whiten(x_ref[...], live, tab_ref, band_ref[...])

    pl.semaphore_wait(barrier, Z - 1 + YC - 1 + has_left.astype(jnp.int32))
    for step in range(1, YC):
        signal(ready_sem, device(x, z, lax.rem(yc + step, YC)))

    own = pltpu.make_async_copy(w_ref.at[me], near_ref.at[me], local_sem.at[6])
    own.start()
    order = (0, 1, 7, 2, 6, 3, 5, 4)

    def send(to_z, to_yc):
        pltpu.make_async_remote_copy(
            src_ref=w_ref.at[to_z * YC + to_yc], dst_ref=near_ref.at[me], send_sem=send_sem,
            recv_sem=near_sem.at[z], device_id=device(x, to_z, to_yc), device_id_type=MESH,
        ).start()

    for step in order[1:]:
        send(lax.rem(z + step, Z), yc)
    for step in range(1, YC):
        send(z, lax.rem(yc + step, YC))
    pl.semaphore_wait(ready_sem, YC - 1)
    for step in order[1:]:
        to_z = lax.rem(z + step, Z)

        def send_on(i, _, to_z=to_z):
            send(to_z, lax.rem(yc + i, YC))
            return 0

        lax.fori_loop(1, YC, send_on, 0)

    @pl.when(jnp.logical_not(has_right))
    def _():
        far_ref[...] = jnp.zeros_like(far_ref)
        far_rest_ref[...] = jnp.zeros_like(far_rest_ref)

    own.wait()
    for step in order:
        from_z = lax.rem(z + Z - step, Z)
        chunk = pl.ds(from_z * YC, YC)
        some = near_ref.at[pl.ds(0, YC if step else YC - 1)]
        pltpu.make_async_copy(some, some, near_sem.at[from_z]).wait()

        @pl.when(jnp.logical_and(has_left, lax.rem(from_z, Z_LO) != Z_LO - 1))
        def _(chunk=chunk):
            pltpu.make_async_remote_copy(
                src_ref=near_ref.at[chunk], dst_ref=far_ref.at[chunk], send_sem=send_sem,
                recv_sem=far_sem, device_id=device(x - 1, z, yc), device_id_type=MESH,
            ).start()

    @pl.when(has_left)
    def _():
        gather_rest(near_ref, near_rest_ref)
        pltpu.make_async_remote_copy(
            src_ref=near_rest_ref, dst_ref=far_rest_ref, send_sem=send_sem,
            recv_sem=rest_sem, device_id=device(x - 1, z, yc), device_id_type=MESH,
        ).start()

    def give(start, end):
        round_rows(u_ref, s_ref, start, end)
        first, count = start // 2, (end - start) // 2

        def go(i, _):
            pair = first + lax.rem(i + z * 2 + yc, count)
            to_z = lax.div(lax.rem(pair, 2 * YC), YC) * Z_LO + lax.div(pair, 2 * YC)
            to_yc = lax.rem(pair, YC)

            @pl.when(to_z * YC + to_yc != me)
            def _():
                pltpu.make_async_remote_copy(
                    src_ref=s_ref.at[pair], dst_ref=got_ref.at[me], send_sem=send_sem,
                    recv_sem=got_sem, device_id=device(x, to_z, to_yc), device_id_type=MESH,
                ).start()
            return 0

        lax.fori_loop(0, count, go, 0, unroll=2)

    regroup_plane(near_ref, t_ref, 0)
    near_pairs(t_ref, u_ref, left_ref)
    give(0, EARLY)

    @pl.when(has_right)
    def _():
        whole = far_ref.at[pl.ds(0, 2 * (Z_LO - 1) * YC)]
        pltpu.make_async_copy(whole, whole, far_sem).wait()
        pltpu.make_async_copy(far_rest_ref, far_rest_ref, rest_sem).wait()

    regroup_plane(far_ref, t_ref, 1, far_rest_ref)
    for start, send_start, end in BLOCKS:
        far_pairs(t_ref, u_ref, left_ref, both_ref, start, end, start == BLOCKS[0][0])
        give(send_start, end)

    owned = lax.rem(z, Z_LO) * (2 * YC) + lax.div(z, Z_LO) * YC + yc
    own = pltpu.make_async_copy(s_ref.at[owned], got_ref.at[me], local_sem.at[7])
    own.start()
    own.wait()
    loads[4].wait()
    loads[5].wait()
    rest = got_ref.at[pl.ds(0, PLANE - 1)]
    pltpu.make_async_copy(rest, rest, got_sem).wait()

    right = jnp.concatenate([got_ref[:, c].reshape(SAMPLES, LANES) for c in range(2)], axis=1)
    pairs = dot(itab_ref[0], right, ((1,), (0,)))
    for term in range(1, itab_ref.shape[0]):
        pairs = pairs + dot(itab_ref[term], right, ((1,), (0,)))
    offsets = lax.broadcasted_iota(jnp.int32, (LAGS_PAD, LANES), 1) + 1
    first = lax.rem(chan, Z_LO) * 32 + win * 2
    for c in range(2):
        reach = jnp.minimum(limit_ref[win * 2 + c], CHANNELS - 1 - (chan * 32 + win * 2 + c))
        kept = pltpu.roll(pairs[:, c * LANES:(c + 1) * LANES], LANES - 1 - c - first, 1)
        out_ref[pl.ds(c, LAGS_PAD - 8, stride=2)] = jnp.where(offsets <= reach, kept, 0.0)[:LAGS_PAD - 8]

    sent = w_ref.at[pl.ds(0, PLANE - 1)]
    pltpu.make_async_copy(sent, sent, send_sem).wait()
    pltpu.make_async_copy(rest, rest, send_sem).wait()

    @pl.when(has_left)
    def _():
        whole = far_ref.at[pl.ds(0, 2 * (Z_LO - 1) * YC)]
        pltpu.make_async_copy(whole, whole, send_sem).wait()
        pltpu.make_async_copy(near_rest_ref, near_rest_ref, send_sem).wait()


def shards(records, live, band_limit):
    tab = jnp.asarray(forward_tables(2))
    band = jnp.asarray(band_table())
    itab = jnp.asarray(inverse_tables(2))
    rows = records.reshape(LANES, SAMPLES)
    vmem, hbm = pl.BlockSpec(memory_space=pltpu.VMEM), pl.BlockSpec(memory_space=pltpu.HBM)
    out = pl.pallas_call(
        kernel,
        out_shape=jax.ShapeDtypeStruct((2 * LAGS_PAD, LANES), F32),
        in_specs=[hbm] * 6,
        out_specs=vmem,
        scratch_shapes=[
            pltpu.SMEM(band_limit.shape, jnp.int32),
            pltpu.SMEM(live.shape, jnp.int32),
            pltpu.VMEM(rows.shape, BF16),
            pltpu.VMEM(tab.shape, BF16),
            pltpu.VMEM(band.shape, BF16),
            pltpu.VMEM(itab.shape, BF16),
            pltpu.VMEM((PLANE, ROWS, LANES), BF16),
            pltpu.VMEM((PLANE, ROWS, LANES), BF16),
            pltpu.VMEM((PLANE, ROWS, LANES), BF16),
            pltpu.VMEM((2, ROWS, LANES), BF16),
            pltpu.VMEM((2, ROWS, LANES), BF16),
            pltpu.VMEM((2, 2, (WINS_ALL + 1) * SLICE, LANES), F32),
            pltpu.VMEM(((LANES + 1) * ROWS, LANES), F32),
            pltpu.VMEM((SLICE, LANES, LANES), BF16),
            pltpu.VMEM((SLICE, LANES, 2 * LANES), BF16),
            pltpu.VMEM((PLANE, 2, ROWS, LANES), BF16),
            pltpu.VMEM((PLANE, 2, ROWS, LANES), BF16),
            pltpu.SemaphoreType.DMA((8,)),
            pltpu.SemaphoreType.DMA,
            pltpu.SemaphoreType.DMA((Z,)),
            pltpu.SemaphoreType.DMA,
            pltpu.SemaphoreType.DMA,
            pltpu.SemaphoreType.DMA,
            pltpu.SemaphoreType.REGULAR,
        ],
        compiler_params=pltpu.CompilerParams(
            collective_id=0, has_side_effects=True, vmem_limit_bytes=40 << 20
        ),
        cost_estimate=pl.CostEstimate(flops=1_500_000_000, bytes_accessed=8_000_000, transcendentals=65536),
        name="correlate",
    )(*[pltpu.with_memory_space_constraint(a, pltpu.HBM) for a in (band_limit, live, rows, tab, band, itab)])
    out = out.reshape(LAGS_PAD, 2, LANES)[:LAGS, :, :R]
    return jnp.transpose(out, (1, 2, 0))


def solution(mesh):
    placed = (P("win", "chan", None), P("chan"), P("chan"))
    return jax.shard_map(
        shards,
        mesh=mesh,
        in_specs=placed,
        out_specs=P(("chan", "win"), None, None),
        check_vma=False,
    )
```

```python
import math

import jax
import jax.numpy as jnp
import ml_dtypes
import numpy as np
from jax import lax
from jax.experimental import pallas as pl
from jax.experimental.pallas import tpu as pltpu
from jax.sharding import PartitionSpec as P

R = 100
LANES = 128
HALF_LAG = 128
HALF_WIN = 32
SAMPLES = 1024
BINS = SAMPLES // 2
LAGS = 2 * HALF_LAG + 1
WINS_ALL = 64
CHANNELS = 512

LAGS_PAD = 272
X, Z_LO, Z, YC = 4, 4, 8, 8
PLANE = Z * YC
SLICE = BINS // PLANE
EARLY = (LANES - R) // 4 * 4
BLOCKS = ((16, EARLY, 64), (64, 64, 96), (96, 96, 128))
ROWS = 2 * SLICE
REST = R - (Z_LO - 1) * 32

MESH = pl.DeviceIdType.MESH
F32, BF16 = jnp.float32, jnp.bfloat16


def split(table, terms):
    parts, rest = [], table.astype(np.float64)
    for _ in range(terms):
        part = rest.astype(np.float32).astype(ml_dtypes.bfloat16)
        parts.append(part)
        rest = rest - part.astype(np.float64)
    return parts


RESIDUES = (0, 4, 1, 7, 2, 6, 3, 5)
RUN = BINS // 8
ORDER = np.concatenate([np.arange(RUN) * 8 + (r or 8) for r in RESIDUES])


def forward_tables(terms):
    groups = []
    for g in range(4):
        halves = []
        for side in range(2):
            freqs = ORDER[(2 * g + side) * RUN:(2 * g + side + 1) * RUN, None]
            phase = np.mod(freqs * np.arange(LANES)[None, :], SAMPLES) * (2.0 * math.pi / SAMPLES)
            cos, sin = np.cos(phase), np.sin(phase)
            if g == 0:
                real, imag = [np.zeros_like(cos)] * 2, [np.zeros_like(cos)] * 2
                real[side], imag[side] = cos, -sin
            else:
                sign = 1 - 2 * side
                real, imag = [cos, sign * sin], [-sin, sign * cos]
            halves.append((np.concatenate(real, axis=1), np.concatenate(imag, axis=1)))
        (real_a, imag_a), (real_b, imag_b) = halves
        groups.append(np.concatenate([real_a, real_b, imag_a, imag_b], axis=0))
    return np.stack(split(np.stack(groups), terms))


def inverse_tables(terms):
    freqs = ORDER[:, None]
    shifts = np.arange(LAGS)[None, :] - HALF_LAG
    phase = np.mod(freqs * shifts, SAMPLES) * (2.0 * math.pi / SAMPLES)
    factor = 2.0 / math.sqrt(SAMPLES * WINS_ALL)
    real = (np.cos(phase) * factor).reshape(PLANE, SLICE, LAGS)
    imag = (-np.sin(phase) * factor).reshape(PLANE, SLICE, LAGS)
    table = np.concatenate([real, imag], axis=1).reshape(SAMPLES, LAGS).T
    table = np.pad(table, ((0, LAGS_PAD - LAGS), (0, 0)))
    return np.stack(split(table, terms))


def band_table():
    return (np.abs(ORDER[:, None] - ORDER[None, :]) <= HALF_WIN).astype(ml_dtypes.bfloat16)


def dot(a, b, dims):
    return lax.dot_general(a, b, (dims, ((), ())), preferred_element_type=F32)


def residue_sums(x):
    b = [x[:, LANES * i:LANES * (i + 1)].astype(F32) for i in range(8)]
    plus = [b[i] + b[i + 4] for i in range(4)]
    minus = [b[i] - b[i + 4] for i in range(4)]
    even, odd = plus[0] + plus[2], plus[1] + plus[3]
    root = math.sqrt(0.5)
    across, along = (minus[1] - minus[3]) * root, (minus[1] + minus[3]) * root
    return (
        (even + odd, even - odd),
        (minus[0] + across, -minus[2] - along),
        (plus[0] - plus[2], plus[3] - plus[1]),
        (minus[0] - across, minus[2] - along),
    )


def whiten(x, live, tab_ref, band):
    real, imag = [], []
    for g, sums in enumerate(residue_sums(x)):
        sums = jnp.concatenate(sums, axis=1)
        high = sums.astype(BF16)
        low = (sums - high.astype(F32)).astype(BF16)
        spec = dot(tab_ref[0, g], high, ((1,), (1,)))
        spec = spec + dot(tab_ref[0, g], low, ((1,), (1,)))
        spec = spec + dot(tab_ref[1, g], high, ((1,), (1,)))
        real.append(spec[:2 * RUN])
        imag.append(spec[2 * RUN:])
    real, imag = jnp.concatenate(real, axis=0), jnp.concatenate(imag, axis=0)
    amplitude = jnp.sqrt(real * real + imag * imag)
    high = amplitude.astype(BF16)
    low = (amplitude - high.astype(F32)).astype(BF16)
    near = dot(band, high, ((1,), (0,))) + dot(band, low, ((1,), (0,)))
    factor = live / (near * (1.0 / (2 * HALF_WIN + 1)) + 1e-06)
    real = (real * factor).reshape(PLANE, SLICE, LANES)
    imag = (imag * factor).reshape(PLANE, SLICE, LANES)
    return jnp.concatenate([real, imag], axis=1).astype(BF16)


def regroup(parts):
    group = lax.broadcasted_iota(jnp.int32, parts[0].shape, 1) // 32
    for bit in range(2):
        step = 32 << bit
        upper = (group // (1 << bit)) % 2 == 1
        new = list(parts)
        for i in range(4):
            if i & (1 << bit):
                continue
            a, b = parts[i], parts[i | (1 << bit)]
            new[i] = jnp.where(upper, pltpu.roll(b, step, 1), a)
            new[i | (1 << bit)] = jnp.where(upper, b, pltpu.roll(a, LANES - step, 1))
        parts = new
    return parts


def regroup_plane(ref, t_ref, plane, rest_ref=None):
    def take(s, _):
        from_z = lax.div(s, YC) * (Z_LO * YC) + lax.rem(s, YC)
        if rest_ref is None:
            parts = [ref[from_z + z * YC] for z in range(Z_LO)]
        else:
            parts = [ref[from_z + z * YC] for z in range(Z_LO - 1)]
            shift = lax.rem(LANES - REST * lax.rem(s, YC), LANES)
            parts.append(pltpu.roll(rest_ref[lax.div(s, YC)], shift, 1))
        parts = [part.astype(F32) for part in regroup(parts)]
        for w in range(4):
            at = pl.ds(pl.multiple_of((s * 4 + w) * SLICE, SLICE), SLICE)
            t_ref[plane, 0, at] = parts[w][:SLICE]
            t_ref[plane, 1, at] = parts[w][SLICE:]
        return 0

    lax.fori_loop(0, 2 * YC, take, 0, unroll=16)


def columns(t_ref, plane, f):
    every = pl.ds(f, WINS_ALL, stride=SLICE)
    re, im = t_ref[plane, 0, every], t_ref[plane, 1, every]
    own = jnp.concatenate([re, im], axis=0)
    turned = jnp.concatenate([-im, re], axis=0)
    return own, jnp.concatenate([own, turned], axis=1).astype(BF16)


def gather_rest(near_ref, rest_ref):
    place = lax.broadcasted_iota(jnp.int32, (ROWS, LANES), 1) % 32 // REST
    for high in range(2):
        first = (high * Z_LO + Z_LO - 1) * YC
        rest = near_ref[first]
        for from_yc in range(1, YC):
            rest = jnp.where(place == from_yc, pltpu.roll(near_ref[first + from_yc], REST * from_yc, 1), rest)
        rest_ref[high] = rest


def near_pairs(t_ref, u_ref, left_ref):
    for f in range(SLICE):
        own, both = columns(t_ref, 0, f)
        left = own.T.astype(BF16)
        left_ref[f] = left
        pairs = dot(left, both, ((1,), (0,)))
        for part in range(2):
            u_ref[pl.ds(part * SLICE + f, LANES, stride=ROWS)] = pairs[:, part * LANES:(part + 1) * LANES]


def far_pairs(t_ref, u_ref, left_ref, both_ref, start, end, first):
    rows = lax.broadcasted_iota(jnp.int32, (end - start, LANES), 0) + start
    near = lax.broadcasted_iota(jnp.int32, (end - start, LANES), 1) > rows
    for f in range(SLICE):
        if first:
            both_ref[f] = columns(t_ref, 1, f)[1]
        pairs = dot(left_ref[f, start:end], both_ref[f], ((1,), (0,)))
        for part in range(2):
            at = pl.ds(start * ROWS + part * SLICE + f, end - start, stride=ROWS)
            u_ref[at] = jnp.where(near, u_ref[at], pairs[:, part * LANES:(part + 1) * LANES])


def round_rows(u_ref, s_ref, start, end):
    done = u_ref[start * ROWS:end * ROWS]
    s_ref[start // 2:end // 2] = done.astype(BF16).reshape((end - start) // 2, 2, ROWS, LANES)


def kernel(limit_hbm, live_hbm, x_hbm, tab_hbm, band_hbm, itab_hbm, out_ref,
           limit_ref, live_ref, x_ref, tab_ref, band_ref, itab_ref, w_ref, near_ref, far_ref, near_rest_ref, far_rest_ref, t_ref, u_ref, left_ref, both_ref, s_ref, got_ref,
           local_sem, send_sem, near_sem, far_sem, got_sem, rest_sem, ready_sem):
    chan, win = lax.axis_index("chan"), lax.axis_index("win")
    x = lax.div(chan, Z_LO)
    z, yc = lax.div(win, YC) * Z_LO + lax.rem(chan, Z_LO), lax.rem(win, YC)
    me = z * YC + yc
    has_left, has_right = x > 0, x < X - 1

    def device(to_x, to_z, to_yc):
        return {"chan": to_x * Z_LO + lax.rem(to_z, Z_LO), "win": lax.div(to_z, Z_LO) * YC + to_yc}

    loads = [
        pltpu.make_async_copy(src, dst, local_sem.at[i])
        for i, (src, dst) in enumerate(
            ((live_hbm, live_ref), (x_hbm, x_ref), (tab_hbm, tab_ref), (band_hbm, band_ref),
             (itab_hbm, itab_ref), (limit_hbm, limit_ref)))
    ]
    for load in loads[:4]:
        load.start()

    barrier = pltpu.get_barrier_semaphore()

    def signal(semaphore, to):
        pl.semaphore_signal(semaphore, inc=1, device_id=to, device_id_type=MESH)

    for step in range(1, Z):
        signal(barrier, device(x, lax.rem(z + step, Z), yc))
    for step in range(1, YC):
        signal(barrier, device(x, z, lax.rem(yc + step, YC)))

    @pl.when(has_right)
    def _():
        signal(barrier, device(x + 1, z, yc))

    for load in loads[4:]:
        load.start()
    lane = lax.rem(lax.broadcasted_iota(jnp.int32, (1, LANES), 1), 32)
    live = jnp.zeros((1, LANES), F32)
    loads[0].wait()
    for c in range(32):
        live = jnp.where(lane == c, live_ref[c].astype(F32), live)
    for load in loads[1:4]:
        load.wait()
    w_ref[...] = whiten(x_ref[...], live, tab_ref, band_ref[...])

    pl.semaphore_wait(barrier, Z - 1 + YC - 1 + has_left.astype(jnp.int32))
    for step in range(1, YC):
        signal(ready_sem, device(x, z, lax.rem(yc + step, YC)))

    own = pltpu.make_async_copy(w_ref.at[me], near_ref.at[me], local_sem.at[6])
    own.start()
    order = (0, 1, 7, 2, 6, 3, 5, 4)

    def send(to_z, to_yc):
        pltpu.make_async_remote_copy(
            src_ref=w_ref.at[to_z * YC + to_yc], dst_ref=near_ref.at[me], send_sem=send_sem,
            recv_sem=near_sem.at[z], device_id=device(x, to_z, to_yc), device_id_type=MESH,
        ).start()

    for step in range(1, YC):
        send(z, lax.rem(yc + step, YC))
    pl.semaphore_wait(ready_sem, YC - 1)
    for step in order[1:]:
        to_z = lax.rem(z + step, Z)

        def send_on(i, _, to_z=to_z):
            send(to_z, lax.rem(yc + i, YC))
            return 0

        lax.fori_loop(0, YC, send_on, 0)

    @pl.when(jnp.logical_not(has_right))
    def _():
        far_ref[...] = jnp.zeros_like(far_ref)
        far_rest_ref[...] = jnp.zeros_like(far_rest_ref)

    own.wait()
    for step in order:
        from_z = lax.rem(z + Z - step, Z)
        chunk = pl.ds(from_z * YC, YC)
        some = near_ref.at[pl.ds(0, YC if step else YC - 1)]
        pltpu.make_async_copy(some, some, near_sem.at[from_z]).wait()

        @pl.when(jnp.logical_and(has_left, lax.rem(from_z, Z_LO) != Z_LO - 1))
        def _(chunk=chunk):
            pltpu.make_async_remote_copy(
                src_ref=near_ref.at[chunk], dst_ref=far_ref.at[chunk], send_sem=send_sem,
                recv_sem=far_sem, device_id=device(x - 1, z, yc), device_id_type=MESH,
            ).start()

    @pl.when(has_left)
    def _():
        gather_rest(near_ref, near_rest_ref)
        pltpu.make_async_remote_copy(
            src_ref=near_rest_ref, dst_ref=far_rest_ref, send_sem=send_sem,
            recv_sem=rest_sem, device_id=device(x - 1, z, yc), device_id_type=MESH,
        ).start()

    def give(start, end):
        round_rows(u_ref, s_ref, start, end)
        first, count = start // 2, (end - start) // 2

        def go(i, _):
            pair = first + lax.rem(i + z * 2 + yc, count)
            to_z = lax.div(lax.rem(pair, 2 * YC), YC) * Z_LO + lax.div(pair, 2 * YC)
            to_yc = lax.rem(pair, YC)

            @pl.when(to_z * YC + to_yc != me)
            def _():
                pltpu.make_async_remote_copy(
                    src_ref=s_ref.at[pair], dst_ref=got_ref.at[me], send_sem=send_sem,
                    recv_sem=got_sem, device_id=device(x, to_z, to_yc), device_id_type=MESH,
                ).start()
            return 0

        lax.fori_loop(0, count, go, 0)

    regroup_plane(near_ref, t_ref, 0)
    near_pairs(t_ref, u_ref, left_ref)
    give(0, EARLY)

    @pl.when(has_right)
    def _():
        whole = far_ref.at[pl.ds(0, 2 * (Z_LO - 1) * YC)]
        pltpu.make_async_copy(whole, whole, far_sem).wait()
        pltpu.make_async_copy(far_rest_ref, far_rest_ref, rest_sem).wait()

    regroup_plane(far_ref, t_ref, 1, far_rest_ref)
    for start, send_start, end in BLOCKS:
        far_pairs(t_ref, u_ref, left_ref, both_ref, start, end, start == BLOCKS[0][0])
        give(send_start, end)

    owned = lax.rem(z, Z_LO) * (2 * YC) + lax.div(z, Z_LO) * YC + yc
    own = pltpu.make_async_copy(s_ref.at[owned], got_ref.at[me], local_sem.at[7])
    own.start()
    own.wait()
    loads[4].wait()
    loads[5].wait()
    rest = got_ref.at[pl.ds(0, PLANE - 1)]
    pltpu.make_async_copy(rest, rest, got_sem).wait()

    right = jnp.concatenate([got_ref[:, c].reshape(SAMPLES, LANES) for c in range(2)], axis=1)
    pairs = dot(itab_ref[0], right, ((1,), (0,)))
    for term in range(1, itab_ref.shape[0]):
        pairs = pairs + dot(itab_ref[term], right, ((1,), (0,)))
    offsets = lax.broadcasted_iota(jnp.int32, (LAGS_PAD, LANES), 1) + 1
    first = lax.rem(chan, Z_LO) * 32 + win * 2
    for c in range(2):
        reach = jnp.minimum(limit_ref[win * 2 + c], CHANNELS - 1 - (chan * 32 + win * 2 + c))
        kept = pltpu.roll(pairs[:, c * LANES:(c + 1) * LANES], LANES - 1 - c - first, 1)
        out_ref[pl.ds(c, LAGS_PAD - 8, stride=2)] = jnp.where(offsets <= reach, kept, 0.0)[:LAGS_PAD - 8]

    sent = w_ref.at[pl.ds(0, PLANE - 1)]
    pltpu.make_async_copy(sent, sent, send_sem).wait()
    pltpu.make_async_copy(rest, rest, send_sem).wait()

    @pl.when(has_left)
    def _():
        whole = far_ref.at[pl.ds(0, 2 * (Z_LO - 1) * YC)]
        pltpu.make_async_copy(whole, whole, send_sem).wait()
        pltpu.make_async_copy(near_rest_ref, near_rest_ref, send_sem).wait()


def shards(records, live, band_limit):
    tab = jnp.asarray(forward_tables(2))
    band = jnp.asarray(band_table())
    itab = jnp.asarray(inverse_tables(2))
    rows = records.reshape(LANES, SAMPLES)
    vmem, hbm = pl.BlockSpec(memory_space=pltpu.VMEM), pl.BlockSpec(memory_space=pltpu.HBM)
    out = pl.pallas_call(
        kernel,
        out_shape=jax.ShapeDtypeStruct((2 * LAGS_PAD, LANES), F32),
        in_specs=[hbm] * 6,
        out_specs=vmem,
        scratch_shapes=[
            pltpu.SMEM(band_limit.shape, jnp.int32),
            pltpu.SMEM(live.shape, jnp.int32),
            pltpu.VMEM(rows.shape, BF16),
            pltpu.VMEM(tab.shape, BF16),
            pltpu.VMEM(band.shape, BF16),
            pltpu.VMEM(itab.shape, BF16),
            pltpu.VMEM((PLANE, ROWS, LANES), BF16),
            pltpu.VMEM((PLANE, ROWS, LANES), BF16),
            pltpu.VMEM((PLANE, ROWS, LANES), BF16),
            pltpu.VMEM((2, ROWS, LANES), BF16),
            pltpu.VMEM((2, ROWS, LANES), BF16),
            pltpu.VMEM((2, 2, (WINS_ALL + 1) * SLICE, LANES), F32),
            pltpu.VMEM(((LANES + 1) * ROWS, LANES), F32),
            pltpu.VMEM((SLICE, LANES, LANES), BF16),
            pltpu.VMEM((SLICE, LANES, 2 * LANES), BF16),
            pltpu.VMEM((PLANE, 2, ROWS, LANES), BF16),
            pltpu.VMEM((PLANE, 2, ROWS, LANES), BF16),
            pltpu.SemaphoreType.DMA((8,)),
            pltpu.SemaphoreType.DMA,
            pltpu.SemaphoreType.DMA((Z,)),
            pltpu.SemaphoreType.DMA,
            pltpu.SemaphoreType.DMA,
            pltpu.SemaphoreType.DMA,
            pltpu.SemaphoreType.REGULAR,
        ],
        compiler_params=pltpu.CompilerParams(
            collective_id=0, has_side_effects=True, vmem_limit_bytes=40 << 20
        ),
        cost_estimate=pl.CostEstimate(flops=1_500_000_000, bytes_accessed=8_000_000, transcendentals=65536),
        name="correlate",
    )(*[pltpu.with_memory_space_constraint(a, pltpu.HBM) for a in (band_limit, live, rows, tab, band, itab)])
    out = out.reshape(LAGS_PAD, 2, LANES)[:LAGS, :, :R]
    return jnp.transpose(out, (1, 2, 0))


def solution(mesh):
    placed = (P("win", "chan", None), P("chan"), P("chan"))
    return jax.shard_map(
        shards,
        mesh=mesh,
        in_specs=placed,
        out_specs=P(("chan", "win"), None, None),
        check_vma=False,
    )
```
